32 devices in a mesh: stretch: 2 (over x), cp: 4 (over z), tp: 4 (over y, core).
Axes of the slice: x: 2, y: 2, z: 4, core: 2. Of those that a mesh axis runs over, the one named last changes fastest.
Arguments:
- query_rows: bfloat16 [4, 512, 6144], P('stretch', 'cp', 'tp'), may hold values from -56 to 56
- key_rows: bfloat16 [4, 512, 6144], P('stretch', 'cp', 'tp'), may hold values from -4 to 4
- value_rows: bfloat16 [4, 512, 6144], P('stretch', 'cp', 'tp'), may hold values from -208 to 208
- gate_table: bfloat16 [16, 6144], P(None, 'tp'), may hold values from 0.5 to 2
- levels: int32 [4], replicated, may hold values from 0 to 15, as said below
- kv_ranges: int32 [2, 4, 4, 4], replicated, may hold values from 0 to 4, as said below
Outputs:
- attention_out: bfloat16 [4, 512, 6144], P('stretch', 'cp', 'tp')
The draws below stay inside these ranges and needn't reach their ends.
Inputs may be any that keep to these rules, and one draw needn't show every extreme that they name: levels[c] lies in [c * 4, (c + 1) * 4), so later stretches are noisier. Write q for a query block, p = 1 and w = [max(0, (q // p - 2) * p), (q // p + 1) * p). Every range has kv_ranges[0] <= kv_ranges[1]. For key stretch c2 > c the range is empty (both 0). For c2 == c it contains block q and lies within w. For c2 < c it is empty (both 0) or lies within w; for c2 == c - 1 it is never empty.
All inputs are finite; a program needn't handle non-finite values.
Results may differ from the reference program's by a relative error of at most 0.0039.
Values may be sent and summed in bfloat16 or wider, within the bound.
No kernel may reach another device: no remote copies, remote signals or barrier semaphores. Data moves between devices by JAX's collectives and lax.ppermute only.
A program may use at most 64 MiB of HBM per device.

```python
import math
import jax
import jax.numpy as jnp
from jax import lax

HEADS = 48
HEAD_DIM = 128
HD = 6144
STRETCHES = 4
TOK_DEV = 128
STRETCH_TOK = 512
BLOCK = 128
BLOCKS = 4
REACH = 2
LEVELS = 16
N_CP = 4


def shared_base(key):
    normal_part = jax.random.normal(key, (STRETCHES, STRETCH_TOK, HD), jnp.float32)
    return normal_part


def draw_key_rows(key, part):
    normal_part = shared_base(key)
    result = jnp.clip(normal_part, -4.0, 4.0)
    return result.astype(jnp.bfloat16)


def draw_query_rows(key, part):
    key = jax.random.fold_in(key, 5)
    result = 2.0 * jnp.clip(jax.random.normal(key, (STRETCHES, STRETCH_TOK, HD), jnp.float32), -4.0, 4.0)
    return result.astype(jnp.bfloat16)


def draw_value_rows(key, part):
    key = jax.random.fold_in(key, 7)
    normal_part = jax.random.normal(key, (STRETCHES, STRETCH_TOK, HD), jnp.float32)
    column_head = (jnp.arange(HD) // HEAD_DIM).astype(jnp.float32) / (HEADS - 1)
    result = jnp.clip(normal_part, -4.0, 4.0) * (10.0 ** column_head)[None, None, :]
    return result.astype(jnp.bfloat16)


def draw_levels(key, part):
    key = jax.random.fold_in(key, 9)
    stride = LEVELS // STRETCHES
    offset = jax.random.randint(key, (STRETCHES,), 0, stride)
    return (jnp.arange(STRETCHES, dtype=jnp.int32) * stride + offset).astype(jnp.int32)


def draw_kv_ranges(key, part):
    key = jax.random.fold_in(key, 13)
    blocks_dev = TOK_DEV // BLOCK
    shape = (STRETCHES, BLOCKS, STRETCHES)
    query_block = jnp.arange(BLOCKS, dtype=jnp.int32)[None, :, None]
    query_stretch = jnp.arange(STRETCHES, dtype=jnp.int32)[:, None, None]
    key_stretch = jnp.arange(STRETCHES, dtype=jnp.int32)[None, None, :]
    device = query_block // blocks_dev
    window_low = jnp.broadcast_to(jnp.maximum(device - REACH, 0) * blocks_dev, shape)
    window_high = jnp.broadcast_to((device + 1) * blocks_dev, shape)
    query_full = jnp.broadcast_to(query_block, shape)
    own_low = window_low + jax.random.randint(jax.random.fold_in(key, 1), shape, 0, query_full - window_low + 1)
    forced = (jax.random.randint(jax.random.fold_in(key, 2), shape, 0, 4) == 0) | (query_full == BLOCKS - 1)
    own_low = jnp.where(forced, window_low, own_low)
    own_high = query_full + 1 + jax.random.randint(jax.random.fold_in(key, 3), shape, 0, window_high - query_full)
    far_low = window_low + jax.random.randint(jax.random.fold_in(key, 4), shape, 0, window_high - window_low)
    far_high = far_low + 1 + jax.random.randint(jax.random.fold_in(key, 5), shape, 0, window_high - far_low)
    keeper = jax.random.randint(jax.random.fold_in(key, 6), shape, 0, 4)
    stretch_gap = jnp.broadcast_to(query_stretch - key_stretch, shape)
    live = (stretch_gap == 1) | (stretch_gap == 2) & (keeper < 2) | (stretch_gap >= 3) & (keeper == 0)
    earlier = (stretch_gap > 0) & live
    low_end = jnp.where(stretch_gap == 0, own_low, jnp.where(earlier, far_low, 0))
    high_end = jnp.where(stretch_gap == 0, own_high, jnp.where(earlier, far_high, 0))
    return jnp.stack([low_end, high_end]).astype(jnp.int32)


def level_of(rng, dims, pieces, low, high):
    def one(dim, blocks):
        heights = jax.random.uniform(jax.random.fold_in(jax.random.fold_in(rng, 6), dim), (blocks,), jnp.float32, low / len(pieces), high / len(pieces))
        return jnp.repeat(jnp.exp(heights), dims[dim] // blocks).reshape((-1,) + (1,) * (len(dims) - dim - 1))

    gain = one(*pieces[0])
    for cut in pieces[1:]:
        gain = gain * one(*cut)
    return gain


def setup_inputs(seed: int = 0) -> dict:
    arg_keys = jax.random.split(jax.random.key(seed), 7)
    return {
        "query_rows": draw_query_rows(jax.random.fold_in(arg_keys[6], 71), 0),
        "key_rows": draw_key_rows(jax.random.fold_in(arg_keys[6], 71), 0),
        "value_rows": draw_value_rows(jax.random.fold_in(arg_keys[6], 71), 0),
        "gate_table": jnp.clip(jnp.exp(math.log(2.0) - 1.3862944 * jax.random.uniform(arg_keys[3], (LEVELS, HD), jnp.float32) ** level_of(arg_keys[3], (LEVELS, HD), ((1, 4),), -0.2, 0.2)), 0.5, 2.0).astype(jnp.bfloat16),
        "levels": draw_levels(jax.random.fold_in(arg_keys[6], 71), 0),
        "kv_ranges": draw_kv_ranges(jax.random.fold_in(arg_keys[6], 71), 0),
    }


def reference(query_rows, key_rows, value_rows, gate_table, levels, kv_ranges):
    blocks_dev = TOK_DEV // BLOCK
    span_rows = (REACH + 1) * TOK_DEV
    score_scale = 1.0 / math.sqrt(HEAD_DIM)
    results = []
    for stretch_index in range(STRETCHES):
        gate_row = gate_table[levels[stretch_index]].astype(jnp.float32)

        def one_block(device, stretch_index=stretch_index, gate_row=gate_row):
            start_row = (jnp.maximum(device - REACH, 0) * TOK_DEV).astype(jnp.int32)
            query_part = lax.dynamic_slice_in_dim(query_rows[stretch_index], (device * TOK_DEV).astype(jnp.int32), TOK_DEV, 0)
            query_part = query_part.astype(jnp.float32).reshape(TOK_DEV, HEADS, HEAD_DIM)
            key_block = (start_row + jnp.arange(span_rows, dtype=jnp.int32)) // BLOCK
            key_list = []
            value_list = []
            mask_list = []
            for source in range(stretch_index + 1):
                key_list.append(lax.dynamic_slice_in_dim(key_rows[source], start_row, span_rows, 0))
                value_list.append(lax.dynamic_slice_in_dim(value_rows[source], start_row, span_rows, 0))
                bounds = lax.dynamic_slice(kv_ranges[:, stretch_index, :, source], (jnp.int32(0), (device * blocks_dev).astype(jnp.int32)), (2, blocks_dev))
                low_tok = jnp.repeat(bounds[0], BLOCK)
                high_tok = jnp.repeat(bounds[1], BLOCK)
                mask_list.append((key_block[None, :] >= low_tok[:, None]) & (key_block[None, :] < high_tok[:, None]))
            key_all = jnp.concatenate(key_list, axis=0).astype(jnp.float32).reshape(-1, HEADS, HEAD_DIM)
            value_all = jnp.concatenate(value_list, axis=0).astype(jnp.float32).reshape(-1, HEADS, HEAD_DIM)
            visible_mask = jnp.concatenate(mask_list, axis=1)[:, None, :]
            scores = jnp.einsum('qhd,khd->qhk', query_part, key_all) * score_scale
            scores = jnp.where(visible_mask, scores, -1e+30)
            peak_score = lax.optimization_barrier(jnp.max(scores, axis=-1, keepdims=True))
            weight = jnp.where(visible_mask, jnp.exp(scores - peak_score), 0.0)
            weight_sum = lax.optimization_barrier(jnp.sum(weight, axis=-1))
            weight_bf = lax.optimization_barrier(weight.astype(jnp.bfloat16)).astype(jnp.float32)
            attended = jnp.einsum('qhk,khd->qhd', weight_bf, value_all) / weight_sum[..., None]
            attended = attended.reshape(TOK_DEV, HEADS * HEAD_DIM)
            mean_square = lax.optimization_barrier(jnp.mean(attended * attended, axis=-1, keepdims=True))
            return (attended * lax.rsqrt(mean_square + 1e-06) * gate_row[None, :]).astype(jnp.bfloat16)
        blocks_out = lax.map(one_block, jnp.arange(N_CP, dtype=jnp.int32))
        results.append(blocks_out.reshape(STRETCH_TOK, HEADS * HEAD_DIM))
    return jnp.stack(results)
```

```python
import functools
import math

import jax
import jax.numpy as jnp
from jax import lax
from jax.experimental import pallas as pl
from jax.experimental.pallas import tpu as pltpu
from jax.sharding import PartitionSpec as P

HEADS = 48
HEAD_DIM = 128
BLOCK = 128
REACH = 2
CHUNKS = (3, 3, 3, 3)
STAT_ROWS = 16
HIDDEN = -1e30
EXPONENT_SCALE = math.log2(math.e) / math.sqrt(HEAD_DIM)


def moved(block, axis, distance):
    devices = range(lax.axis_size(axis))
    route = [(i - distance, i) for i in devices if i - distance in devices]
    return lax.ppermute(block, axis, route)


def head_columns(head):
    return slice(head * HEAD_DIM, (head + 1) * HEAD_DIM)


def stretch_rows(slot):
    return slice(slot * BLOCK, (slot + 1) * BLOCK)


def as_rows(columns):
    return jnp.transpose(columns)[:STAT_ROWS]


def as_columns(rows):
    fill = jnp.zeros((BLOCK - rows.shape[0], BLOCK), jnp.float32)
    return jnp.transpose(jnp.concatenate([rows, fill], axis=0))


def put_stats(payload_ref, stats, token_rows):
    high = stats.astype(jnp.bfloat16)
    rest = stats - high.astype(jnp.float32)
    middle = rest.astype(jnp.bfloat16)
    low = (rest - middle.astype(jnp.float32)).astype(jnp.bfloat16)
    rows = slice(token_rows, token_rows + STAT_ROWS)
    for index, piece in enumerate((high, middle, low)):
        payload_ref[rows, head_columns(index)] = piece


def get_stats(payload_ref, token_rows):
    rows = slice(token_rows, token_rows + STAT_ROWS)
    pieces = [
        payload_ref[rows, head_columns(index)].astype(jnp.float32) for index in range(3)
    ]
    return (pieces[0] + pieces[1]) + pieces[2]


def attend_kernel(
    head_count,
    place_ref,
    ranges_ref,
    own_q,
    near_q,
    far_q,
    own_kv,
    prior_kv,
    own_out,
    own_stats,
    near_out,
    near_stats,
    far_payload,
):
    group, position, stretch_count, block_count = (place_ref[i] for i in range(4))
    pair_count = own_q.shape[0] // BLOCK
    token_rows = pair_count * BLOCK
    value_base = head_count * HEAD_DIM
    high_base = stretch_count * block_count * stretch_count

    def hidden_bias(query_stretch, query_block, key_stretch):
        valid = (key_stretch >= 0) & (query_block < block_count)
        entry = (
            query_stretch * block_count + jnp.minimum(query_block, block_count - 1)
        ) * stretch_count + jnp.maximum(key_stretch, 0)
        visible = (
            valid
            & (ranges_ref[entry] <= position)
            & (position < ranges_ref[high_base + entry])
        )
        return jnp.where(visible, 0.0, HIDDEN)

    lane = lax.broadcasted_iota(jnp.int32, (BLOCK, BLOCK), 1)
    stats = [jnp.zeros((BLOCK, BLOCK), jnp.float32) for _ in range(REACH + 1)]
    biases = {
        (distance, slot): [
            hidden_bias(
                group * pair_count + slot,
                position + distance,
                (group - 1) * pair_count + key_slot,
            )
            for key_slot in range(2 * pair_count)
        ]
        for distance in range(REACH + 1)
        for slot in range(pair_count)
    }
    for head in range(head_count):
        columns = head_columns(head)
        value_columns = slice(value_base + columns.start, value_base + columns.stop)
        keys = jnp.concatenate([prior_kv[:, columns], own_kv[:, columns]], axis=0)
        values = jnp.concatenate(
            [prior_kv[:, value_columns], own_kv[:, value_columns]], axis=0
        )
        for distance, query_ref in ((2, far_q), (1, near_q), (0, own_q)):
            for slot in range(pair_count):
                rows = stretch_rows(slot)
                scores = lax.dot_general(
                    query_ref[rows, columns],
                    keys,
                    (((1,), (1,)), ((), ())),
                    preferred_element_type=jnp.float32,
                )
                scores = jnp.concatenate(
                    [
                        scores[:, stretch_rows(key_slot)] + bias
                        for key_slot, bias in enumerate(biases[distance, slot])
                    ],
                    axis=1,
                )
                peak = jnp.max(scores, axis=1, keepdims=True)
                weight = jnp.exp2((scores - peak) * EXPONENT_SCALE)
                total = jnp.sum(weight, axis=1, keepdims=True)
                summed = jnp.dot(
                    weight.astype(jnp.bfloat16), values, preferred_element_type=jnp.float32
                )
                attended = summed * (1.0 / total)
                log_total = peak * EXPONENT_SCALE + jnp.log2(total)
                stats[distance] = jnp.where(
                    lane == slot * head_count + head, log_total, stats[distance]
                )
                if distance == 0:
                    own_out[rows, columns] = attended
                elif distance == 1:
                    near_out[rows, columns] = attended
                else:
                    far_payload[rows, columns] = attended.astype(jnp.bfloat16)
    own_stats[...] = as_rows(stats[0])
    near_stats[...] = as_rows(stats[1])
    put_stats(far_payload, as_rows(stats[2]), token_rows)


def joined(place_ref, local_out, local_stats, payload_ref, head_count):
    token_rows = local_out.shape[0]
    local_log = local_stats[...]
    remote_log = jnp.where(place_ref[1] > 0, get_stats(payload_ref, token_rows), HIDDEN)
    top = jnp.maximum(local_log, remote_log)
    local_weight = jnp.exp2(local_log - top)
    remote_weight = jnp.exp2(remote_log - top)
    both = local_weight + remote_weight
    scale = 1.0 / both
    columns_of = as_columns(
        jnp.concatenate([local_weight * scale, remote_weight * scale], axis=0)
    )
    parts = {}
    for slot in range(token_rows // BLOCK):
        for head in range(head_count):
            index = slot * head_count + head
            rows, columns = stretch_rows(slot), head_columns(head)
            parts[slot, head] = local_out[rows, columns] * columns_of[
                :, index : index + 1
            ] + payload_ref[rows, columns].astype(jnp.float32) * columns_of[
                :, STAT_ROWS + index : STAT_ROWS + index + 1
            ]
    return parts, top + jnp.log2(both)


def relay_kernel(head_count, place_ref, local_out, local_stats, payload_in, payload_out):
    parts, log_total = joined(place_ref, local_out, local_stats, payload_in, head_count)
    for (slot, head), part in parts.items():
        payload_out[stretch_rows(slot), head_columns(head)] = part.astype(jnp.bfloat16)
    put_stats(payload_out, log_total, local_out.shape[0])


def finish_kernel(
    head_count, place_ref, local_out, local_stats, payload_in, squares_in, out, squares_out
):
    parts, _ = joined(place_ref, local_out, local_stats, payload_in, head_count)
    lane = lax.broadcasted_iota(jnp.int32, (BLOCK, BLOCK), 1)
    squares = jnp.zeros((BLOCK, BLOCK), jnp.float32)
    for slot in range(local_out.shape[0] // BLOCK):
        total = jnp.zeros((BLOCK, HEAD_DIM), jnp.float32)
        for head in range(head_count):
            part = parts[slot, head]
            out[stretch_rows(slot), head_columns(head)] = part
            total = total + part * part
        total = jnp.sum(total, axis=1, keepdims=True)
        squares = jnp.where(lane == slot, total, squares)
    squares_out[...] = squares_in[...] + jnp.transpose(squares)[: squares_out.shape[0]]


def scale_kernel(head_counts, feature_count, place_ref, levels_ref, squares, gate_table, *refs):
    parts, out = refs[:-1], refs[-1]
    factors = as_columns(lax.rsqrt(squares[...] / feature_count + 1e-06))
    pair_count = out.shape[0] // BLOCK
    gates = gate_table[...].astype(jnp.float32)
    level_ids = lax.broadcasted_iota(jnp.int32, gates.shape, 0)
    for slot in range(pair_count):
        level = levels_ref[place_ref[0] * pair_count + slot]
        gate_row = jnp.sum(jnp.where(level_ids == level, gates, 0.0), axis=0, keepdims=True)
        rows = stretch_rows(slot)
        factor = factors[:, slot : slot + 1]
        base = 0
        for part, head_count in zip(parts, head_counts):
            for head in range(head_count):
                columns = head_columns(base + head)
                out[rows, columns] = (
                    part[rows, head_columns(head)] * factor * gate_row[:, columns]
                ).astype(jnp.bfloat16)
            base += head_count


SMEM = pl.BlockSpec(memory_space=pltpu.SMEM)
VMEM = pl.BlockSpec(memory_space=pltpu.VMEM)
PARAMS = pltpu.CompilerParams(vmem_limit_bytes=32 * 1024 * 1024)


def on_device(query_rows, key_rows, value_rows, gate_table, levels, kv_ranges):
    pair_count, row_count, width_dev = query_rows.shape
    assert row_count == BLOCK
    token_rows = pair_count * row_count
    head_total = width_dev // HEAD_DIM
    group = lax.axis_index("stretch")
    position = lax.axis_index("cp")
    place = jnp.stack(
        [group, position, jnp.int32(kv_ranges.shape[1]), jnp.int32(kv_ranges.shape[2])]
    ).astype(jnp.int32)
    ranges = kv_ranges.reshape(-1)
    queries, keys, values = (
        array.reshape(token_rows, width_dev) for array in (query_rows, key_rows, value_rows)
    )
    head_counts = CHUNKS
    assert sum(head_counts) == head_total
    starts = [sum(head_counts[:i]) * HEAD_DIM for i in range(len(head_counts))]
    widths = [count * HEAD_DIM for count in head_counts]
    chunks = range(len(head_counts))

    def cut(array, chunk):
        return lax.slice_in_dim(array, starts[chunk], starts[chunk] + widths[chunk], axis=1)

    own_q = [cut(queries, i) for i in chunks]
    own_kv = [jnp.concatenate([cut(keys, i), cut(values, i)], axis=1) for i in chunks]
    near_q = [moved(own_q[i], "cp", -1) for i in chunks]
    prior_kv = [moved(own_kv[i], "stretch", 1) for i in chunks]
    far_q = [moved(near_q[i], "cp", -1) for i in chunks]

    def stats_shape():
        return jax.ShapeDtypeStruct((STAT_ROWS, BLOCK), jnp.float32)

    squares = jnp.zeros((8, BLOCK), jnp.float32)
    finished = []
    for i in chunks:
        head_count, width = head_counts[i], widths[i]
        float_shape = jax.ShapeDtypeStruct((token_rows, width), jnp.float32)
        payload_shape = jax.ShapeDtypeStruct((token_rows + STAT_ROWS, width), jnp.bfloat16)
        own_out, own_stats, near_out, near_stats, far_payload = pl.pallas_call(
            functools.partial(attend_kernel, head_count),
            out_shape=(float_shape, stats_shape(), float_shape, stats_shape(), payload_shape),
            in_specs=[SMEM, SMEM] + [VMEM] * 5,
            out_specs=(VMEM,) * 5,
            compiler_params=PARAMS,
        )(place, ranges, own_q[i], near_q[i], far_q[i], own_kv[i], prior_kv[i])
        arrived = moved(far_payload, "cp", 1)
        relayed = pl.pallas_call(
            functools.partial(relay_kernel, head_count),
            out_shape=payload_shape,
            in_specs=[SMEM] + [VMEM] * 3,
            out_specs=VMEM,
            compiler_params=PARAMS,
        )(place, near_out, near_stats, arrived)
        arrived = moved(relayed, "cp", 1)
        part, squares = pl.pallas_call(
            functools.partial(finish_kernel, head_count),
            out_shape=(float_shape, jax.ShapeDtypeStruct(squares.shape, jnp.float32)),
            in_specs=[SMEM] + [VMEM] * 4,
            out_specs=(VMEM, VMEM),
            compiler_params=PARAMS,
        )(place, own_out, own_stats, arrived, squares)
        finished.append(part)
    squares = lax.psum(squares, "tp")
    out = pl.pallas_call(
        functools.partial(scale_kernel, head_counts, float(HEADS * HEAD_DIM)),
        out_shape=jax.ShapeDtypeStruct((token_rows, width_dev), jnp.bfloat16),
        in_specs=[SMEM, SMEM] + [VMEM] * (2 + len(finished)),
        out_specs=VMEM,
        compiler_params=PARAMS,
    )(place, levels, squares, gate_table, *finished)
    return out.reshape(query_rows.shape)


def solution(mesh):
    in_specs = (
        P("stretch", "cp", "tp"),
        P("stretch", "cp", "tp"),
        P("stretch", "cp", "tp"),
        P(None, "tp"),
        P(),
        P(),
    )
    out_specs = P("stretch", "cp", "tp")
    return jax.shard_map(
        on_device, mesh=mesh, in_specs=in_specs, out_specs=out_specs, check_vma=False
    )
```

```python
import functools
import math

import jax
import jax.numpy as jnp
from jax import lax
from jax.experimental import pallas as pl
from jax.experimental.pallas import tpu as pltpu
from jax.sharding import PartitionSpec as P

HEADS = 48
HEAD_DIM = 128
BLOCK = 128
REACH = 2
CHUNKS = (4, 4)
KEYS_MOVED = 4
FINISH_ORDER = (2, 0, 1)
STAT_ROWS = 16
HIDDEN = -1e30
EXPONENT_SCALE = math.log2(math.e) / math.sqrt(HEAD_DIM)


def moved(block, axis, distance):
    devices = range(lax.axis_size(axis))
    route = [(i - distance, i) for i in devices if i - distance in devices]
    return lax.ppermute(block, axis, route)


def head_columns(head):
    return slice(head * HEAD_DIM, (head + 1) * HEAD_DIM)


def stretch_rows(slot):
    return slice(slot * BLOCK, (slot + 1) * BLOCK)


def as_columns(rows):
    fill = jnp.zeros((BLOCK - rows.shape[0], BLOCK), jnp.float32)
    return jnp.transpose(jnp.concatenate([rows, fill], axis=0))


def put_stats(payload_ref, stats, token_rows):
    high = stats.astype(jnp.bfloat16)
    rest = stats - high.astype(jnp.float32)
    middle = rest.astype(jnp.bfloat16)
    low = (rest - middle.astype(jnp.float32)).astype(jnp.bfloat16)
    rows = slice(token_rows, token_rows + STAT_ROWS)
    for index, piece in enumerate((high, middle, low)):
        payload_ref[rows, head_columns(index)] = piece


def get_stats(payload_ref, token_rows):
    rows = slice(token_rows, token_rows + STAT_ROWS)
    pieces = [
        payload_ref[rows, head_columns(index)].astype(jnp.float32) for index in range(3)
    ]
    return (pieces[0] + pieces[1]) + pieces[2]


def shown(place_ref, ranges_ref, query_stretch, query_block, key_stretch, key_block):
    stretch_count, block_count = place_ref[2], place_ref[3]
    low, high = (
        ranges_ref[
            end,
            jnp.minimum(query_stretch, stretch_count - 1),
            jnp.minimum(query_block, block_count - 1),
            jnp.maximum(key_stretch, 0),
        ]
        for end in range(2)
    )
    exists = (
        (query_stretch < stretch_count)
        & (query_block < block_count)
        & (key_stretch >= 0)
        & (key_block >= 0)
    )
    return exists & (low <= key_block) & (key_block < high)


def attend(query, keys, values, seen):
    scores = lax.dot_general(
        keys, query, (((1,), (1,)), ((), ())), preferred_element_type=jnp.float32
    )
    blocks = [scores[stretch_rows(j)] for j in range(len(seen))]
    peak = jnp.full((1, BLOCK), HIDDEN, jnp.float32)
    for block, flag in zip(blocks, seen):
        block_peak = jnp.max(block, axis=0, keepdims=True)
        peak = jnp.maximum(peak, jnp.where(flag, block_peak, HIDDEN))
    shift = peak * EXPONENT_SCALE
    weights = [
        jnp.exp2(block * EXPONENT_SCALE - jnp.where(flag, shift, -HIDDEN))
        for block, flag in zip(blocks, seen)
    ]
    total = sum(jnp.sum(weight, axis=0, keepdims=True) for weight in weights)
    weights = jnp.concatenate([weight.astype(jnp.bfloat16) for weight in weights], axis=0)
    summed = jnp.dot(values, weights, preferred_element_type=jnp.float32)
    total = jnp.maximum(total, 1e-30)
    return summed * (1.0 / total), jnp.maximum(shift + jnp.log2(total), HIDDEN)


def keys_and_values(refs, head, head_count):
    columns = head_columns(head)
    value_columns = head_columns(head_count + head)
    keys = jnp.concatenate([ref[:, columns] for ref in refs], axis=0)
    values = jnp.concatenate([ref[:, value_columns] for ref in refs], axis=0)
    return keys, jnp.transpose(values)


def queries_moved_kernel(
    head_count,
    place_ref,
    ranges_ref,
    own_q,
    near_q,
    far_q,
    own_kv,
    prior_kv,
    *rest,
    pair_count,
):
    own_out, own_stats, near_out, near_stats, far_payload = rest[-5:]
    group, position = place_ref[0], place_ref[1]
    token_rows = pair_count * BLOCK
    seen = {
        (distance, slot): [
            shown(
                place_ref,
                ranges_ref,
                group * pair_count + slot,
                position + distance,
                (group - 1) * pair_count + key_slot,
                position,
            )
            for key_slot in range(2 * pair_count)
        ]
        for distance in range(REACH + 1)
        for slot in range(pair_count)
    }
    own_stats[...] = jnp.zeros_like(own_stats)
    near_stats[...] = jnp.zeros_like(near_stats)
    far_stats = [jnp.zeros((1, BLOCK), jnp.float32)] * STAT_ROWS
    for head in range(head_count):
        columns = head_columns(head)
        keys, values = keys_and_values((prior_kv, own_kv), head, head_count)
        for distance, query_ref in ((2, far_q), (1, near_q), (0, own_q)):
            for slot in range(pair_count):
                rows = stretch_rows(slot)
                attended, log_total = attend(
                    query_ref[rows, columns], keys, values, seen[distance, slot]
                )
                index = slot * head_count + head
                if distance == 0:
                    own_out[rows, columns] = attended
                    own_stats[index : index + 1, :] = log_total
                elif distance == 1:
                    near_out[rows, columns] = attended
                    near_stats[index : index + 1, :] = log_total
                else:
                    far_payload[rows, columns] = attended.astype(jnp.bfloat16)
                    far_stats[index] = log_total
    put_stats(far_payload, jnp.concatenate(far_stats, axis=0), token_rows)


def keys_moved_kernel(
    head_count,
    place_ref,
    ranges_ref,
    own_q,
    next_q,
    own_kv,
    near_kv,
    far_kv,
    *rest,
    pair_count,
):
    own_out, own_stats, next_payload = rest[-3:]
    group, position = place_ref[0], place_ref[1]
    token_rows = pair_count * BLOCK
    seen = {
        (ahead, slot): [
            shown(
                place_ref,
                ranges_ref,
                (group + ahead) * pair_count + slot,
                position,
                group * pair_count + key_slot,
                position - distance,
            )
            for distance in range(REACH + 1)
            for key_slot in range(pair_count)
        ]
        for ahead in range(2)
        for slot in range(pair_count)
    }
    own_stats[...] = jnp.zeros_like(own_stats)
    next_stats = [jnp.zeros((1, BLOCK), jnp.float32)] * STAT_ROWS
    for head in range(head_count):
        columns = head_columns(head)
        keys, values = keys_and_values((own_kv, near_kv, far_kv), head, head_count)
        for ahead, query_ref in ((1, next_q), (0, own_q)):
            for slot in range(pair_count):
                rows = stretch_rows(slot)
                attended, log_total = attend(
                    query_ref[rows, columns], keys, values, seen[ahead, slot]
                )
                index = slot * head_count + head
                if ahead:
                    next_payload[rows, columns] = attended.astype(jnp.bfloat16)
                    next_stats[index] = log_total
                else:
                    own_out[rows, columns] = attended
                    own_stats[index : index + 1, :] = log_total
    put_stats(next_payload, jnp.concatenate(next_stats, axis=0), token_rows)


def joined(sender_index, local_out, local_stats, payload_ref, head_count):
    token_rows = local_out.shape[0]
    local_log = local_stats[...]
    remote_log = jnp.where(sender_index > 0, get_stats(payload_ref, token_rows), HIDDEN)
    top = jnp.maximum(local_log, remote_log)
    local_weight = jnp.exp2(local_log - top)
    remote_weight = jnp.exp2(remote_log - top)
    both = local_weight + remote_weight
    scale = 1.0 / both
    local_weight = local_weight * scale
    remote_weight = remote_weight * scale
    parts = {}
    for slot in range(token_rows // BLOCK):
        for head in range(head_count):
            index = slot * head_count + head
            rows, columns = stretch_rows(slot), head_columns(head)
            parts[slot, head] = (
                local_out[rows, columns] * local_weight[index : index + 1]
                + payload_ref[rows, columns].astype(jnp.float32)
                * remote_weight[index : index + 1]
            )
    return parts, top + jnp.log2(both)


def relay_kernel(
    head_count, place_ref, local_out, local_stats, payload_in, *rest, axis
):
    payload_out = rest[-1]
    parts, log_total = joined(place_ref[axis], local_out, local_stats, payload_in, head_count)
    for (slot, head), part in parts.items():
        payload_out[stretch_rows(slot), head_columns(head)] = part.astype(jnp.bfloat16)
    put_stats(payload_out, log_total, local_out.shape[0])


def finish_kernel(
    head_count, place_ref, local_out, local_stats, payload_in, squares_in, *rest, axis
):
    out, squares_out = rest[-2:]
    parts, _ = joined(place_ref[axis], local_out, local_stats, payload_in, head_count)
    squares_out[...] = squares_in[...]
    for slot in range(local_out.shape[0] // BLOCK):
        total = jnp.zeros((1, BLOCK), jnp.float32)
        for head in range(head_count):
            part = parts[slot, head]
            total = total + jnp.sum(part * part, axis=0, keepdims=True)
            out[stretch_rows(slot), head_columns(head)] = jnp.transpose(part)
        squares_out[slot : slot + 1, :] += total


def scale_kernel(head_counts, feature_count, place_ref, levels_ref, squares, gate_table, *refs):
    parts, out = refs[:-1], refs[-1]
    factors = as_columns(lax.rsqrt(squares[...] / feature_count + 1e-06))
    pair_count = out.shape[0] // BLOCK
    gates = gate_table[...].astype(jnp.float32)
    level_ids = lax.broadcasted_iota(jnp.int32, gates.shape, 0)
    for slot in range(pair_count):
        level = levels_ref[place_ref[0] * pair_count + slot]
        gate_row = jnp.sum(jnp.where(level_ids == level, gates, 0.0), axis=0, keepdims=True)
        rows = stretch_rows(slot)
        factor = factors[:, slot : slot + 1]
        base = 0
        for part, head_count in zip(parts, head_counts):
            for head in range(head_count):
                columns = head_columns(base + head)
                out[rows, columns] = (
                    part[rows, head_columns(head)] * factor * gate_row[:, columns]
                ).astype(jnp.bfloat16)
            base += head_count


def cost(microseconds):
    return pl.CostEstimate(
        flops=int(microseconds * 1e9), bytes_accessed=int(microseconds * 1e6), transcendentals=0
    )


SMEM = pl.BlockSpec(memory_space=pltpu.SMEM)
VMEM = pl.BlockSpec(memory_space=pltpu.VMEM)
PARAMS = pltpu.CompilerParams(vmem_limit_bytes=32 * 1024 * 1024)


def on_device(query_rows, key_rows, value_rows, gate_table, levels, kv_ranges):
    pair_count, row_count, width_dev = query_rows.shape
    assert row_count == BLOCK
    token_rows = pair_count * row_count
    head_total = width_dev // HEAD_DIM
    place = jnp.stack(
        [
            lax.axis_index("stretch"),
            lax.axis_index("cp"),
            jnp.int32(kv_ranges.shape[1]),
            jnp.int32(kv_ranges.shape[2]),
        ]
    ).astype(jnp.int32)
    queries, keys, values = (
        array.reshape(token_rows, width_dev) for array in (query_rows, key_rows, value_rows)
    )
    head_counts = CHUNKS + (KEYS_MOVED,)
    assert sum(head_counts) == head_total
    starts = [sum(head_counts[:i]) * HEAD_DIM for i in range(len(head_counts))]
    widths = [count * HEAD_DIM for count in head_counts]
    chunks = range(len(CHUNKS))
    last = len(CHUNKS)

    def cut(array, chunk):
        return lax.slice_in_dim(array, starts[chunk], starts[chunk] + widths[chunk], axis=1)

    def cut_kv(chunk):
        return jnp.concatenate([cut(keys, chunk), cut(values, chunk)], axis=1)

    def float_shape(chunk):
        return jax.ShapeDtypeStruct((token_rows, widths[chunk]), jnp.float32)

    def payload_shape(chunk):
        return jax.ShapeDtypeStruct((token_rows + STAT_ROWS, widths[chunk]), jnp.bfloat16)

    stats_shape = jax.ShapeDtypeStruct((STAT_ROWS, BLOCK), jnp.float32)
    squares_shape = jax.ShapeDtypeStruct((8, BLOCK), jnp.float32)

    def run(kernel, chunk, microseconds, out_shape, smem, vmem, after=()):
        return pl.pallas_call(
            functools.partial(kernel, head_counts[chunk]),
            out_shape=out_shape,
            in_specs=[SMEM] * len(smem)
            + [VMEM] * len(vmem)
            + [pl.BlockSpec(memory_space=pl.ANY)] * len(after),
            out_specs=(VMEM,) * len(out_shape),
            compiler_params=PARAMS,
            cost_estimate=cost(microseconds),
        )(*smem, *vmem, *after)

    own_q = [cut(queries, i) for i in chunks]
    own_kv = [cut_kv(i) for i in chunks]
    near_q = [moved(own_q[i], "cp", -1) for i in chunks]
    first_q = cut(queries, last)
    first_kv = cut_kv(last)
    near_kv = moved(first_kv, "cp", 1)
    next_q = moved(first_q, "stretch", -1)
    prior_kv = [moved(own_kv[i], "stretch", 1) for i in chunks]
    far_q = [moved(near_q[i], "cp", -1) for i in chunks]
    far_kv = moved(near_kv, "cp", 1)

    own_parts, near_parts, arrived = [], [], []
    for i in chunks:
        own_out, own_stats, near_out, near_stats, far_payload = run(
            functools.partial(queries_moved_kernel, pair_count=pair_count),
            i,
            1.0 * head_counts[i],
            (float_shape(i), stats_shape, float_shape(i), stats_shape, payload_shape(i)),
            (place, kv_ranges),
            (own_q[i], near_q[i], far_q[i], own_kv[i], prior_kv[i]),
        )
        own_parts.append((own_out, own_stats))
        near_parts.append((near_out, near_stats))
        arrived.append(moved(far_payload, "cp", 1))
    own_out, own_stats, next_payload = run(
        functools.partial(keys_moved_kernel, pair_count=pair_count),
        last,
        1.0 * head_counts[last],
        (float_shape(last), stats_shape, payload_shape(last)),
        (place, kv_ranges),
        (first_q, next_q, first_kv, near_kv, far_kv),
    )
    own_parts.append((own_out, own_stats))
    prior_payload = moved(next_payload, "stretch", 1)
    for i in chunks:
        (relayed,) = run(
            functools.partial(relay_kernel, axis=1),
            i,
            0.7,
            (payload_shape(i),),
            (place,),
            (*near_parts[i], arrived[i]),
        )
        arrived[i] = moved(relayed, "cp", 1)
    arrived.append(prior_payload)
    squares = jnp.zeros(squares_shape.shape, jnp.float32)
    finished = [None] * len(head_counts)
    for i in FINISH_ORDER:
        finished[i], squares = run(
            functools.partial(finish_kernel, axis=0 if i == last else 1),
            i,
            0.8,
            (float_shape(i), squares_shape),
            (place,),
            (*own_parts[i], arrived[i], squares),
        )
    squares = lax.psum(squares, "tp")
    out = pl.pallas_call(
        functools.partial(scale_kernel, head_counts, float(HEADS * HEAD_DIM)),
        out_shape=jax.ShapeDtypeStruct((token_rows, width_dev), jnp.bfloat16),
        in_specs=[SMEM, SMEM] + [VMEM] * (2 + len(finished)),
        out_specs=VMEM,
        compiler_params=PARAMS,
    )(place, levels, squares, gate_table, *finished)
    return out.reshape(query_rows.shape)


def solution(mesh):
    in_specs = (
        P("stretch", "cp", "tp"),
        P("stretch", "cp", "tp"),
        P("stretch", "cp", "tp"),
        P(None, "tp"),
        P(),
        P(),
    )
    out_specs = P("stretch", "cp", "tp")
    return jax.shard_map(
        on_device, mesh=mesh, in_specs=in_specs, out_specs=out_specs, check_vma=False
    )
```

```python
import functools
import math

import jax
import jax.numpy as jnp
from jax import lax
from jax.experimental import pallas as pl
from jax.experimental.pallas import tpu as pltpu
from jax.sharding import PartitionSpec as P

HEADS = 48
HEAD_DIM = 128
BLOCK = 128
REACH = 2
CHUNKS = (5, 3)
KEYS_MOVED = 4
FINISH_ORDER = (2, 0, 1)
WRAP = True
NEAR_COST = (3.0, 1.8)
FAR_COST = (1.5, 0.9)
KEYS_COST = 2.0
PACK_LIMIT = 49 * 1024 * 1024
STAT_ROWS = 16
HIDDEN = -1e30
EXPONENT_SCALE = math.log2(math.e) / math.sqrt(HEAD_DIM)


def exchanged(block):
    return lax.ppermute(block, "stretch", [(0, 1), (1, 0)])


def goes_up():
    return lax.axis_index("tp") < lax.axis_size("tp") // 2


def round_trip(block, forward):
    count, half = lax.axis_size("cp"), lax.axis_size("tp") // 2
    route = []
    for lane in range(half):
        cycle = [i * 2 * half + lane for i in range(count)]
        cycle += [i * 2 * half + half + lane for i in reversed(range(count))]
        route += zip(cycle, cycle[1:] + cycle[:1])
    if not forward:
        route = [(target, source) for source, target in route]
    return lax.ppermute(block, ("cp", "tp"), route)


def passed_up(block):
    count = lax.axis_size("cp")
    route = [(i, (i + 1) % count) for i in range(count if WRAP else count - 1)]
    return lax.ppermute(block, "cp", route)


def head_columns(head):
    return slice(head * HEAD_DIM, (head + 1) * HEAD_DIM)


def stretch_rows(slot):
    return slice(slot * BLOCK, (slot + 1) * BLOCK)


def as_columns(rows):
    fill = jnp.zeros((BLOCK - rows.shape[0], BLOCK), jnp.float32)
    return jnp.transpose(jnp.concatenate([rows, fill], axis=0))


def put_stats(payload_ref, stats, token_rows):
    high = stats.astype(jnp.bfloat16)
    rest = stats - high.astype(jnp.float32)
    middle = rest.astype(jnp.bfloat16)
    low = (rest - middle.astype(jnp.float32)).astype(jnp.bfloat16)
    rows = slice(token_rows, token_rows + STAT_ROWS)
    for index, piece in enumerate((high, middle, low)):
        payload_ref[rows, head_columns(index)] = piece


def get_stats(payload_ref, token_rows):
    rows = slice(token_rows, token_rows + STAT_ROWS)
    pieces = [
        payload_ref[rows, head_columns(index)].astype(jnp.float32) for index in range(3)
    ]
    return (pieces[0] + pieces[1]) + pieces[2]


def shown(place_ref, ranges_ref, query_stretch, query_block, key_stretch, key_block):
    stretch_count, block_count = place_ref[2], place_ref[3]
    low, high = (
        ranges_ref[
            end,
            jnp.minimum(query_stretch, stretch_count - 1),
            jnp.minimum(query_block, block_count - 1),
            jnp.maximum(key_stretch, 0),
        ]
        for end in range(2)
    )
    exists = (
        (query_stretch < stretch_count)
        & (query_block < block_count)
        & (key_stretch >= 0)
        & (key_block >= 0)
    )
    return exists & (low <= key_block) & (key_block < high)


def attend(query, keys, values, seen):
    scores = lax.dot_general(
        keys, query, (((1,), (1,)), ((), ())), preferred_element_type=jnp.float32
    )
    blocks = [scores[stretch_rows(j)] for j in range(len(seen))]
    peak = jnp.full((1, BLOCK), HIDDEN, jnp.float32)
    for block, flag in zip(blocks, seen):
        block_peak = jnp.max(block, axis=0, keepdims=True)
        peak = jnp.maximum(peak, jnp.where(flag, block_peak, HIDDEN))
    shift = peak * EXPONENT_SCALE
    weights = [
        jnp.exp2(block * EXPONENT_SCALE - jnp.where(flag, shift, -HIDDEN))
        for block, flag in zip(blocks, seen)
    ]
    total = sum(jnp.sum(weight, axis=0, keepdims=True) for weight in weights)
    weights = jnp.concatenate([weight.astype(jnp.bfloat16) for weight in weights], axis=0)
    summed = jnp.dot(values, weights, preferred_element_type=jnp.float32)
    total = jnp.maximum(total, 1e-30)
    return summed * (1.0 / total), jnp.maximum(shift + jnp.log2(total), HIDDEN)


def pick(up, refs, *index):
    return jnp.where(up, refs[0][index], refs[1][index])


def pack_kernel(counts, keys_moved, place_ref, q_hbm, k_hbm, v_hbm, *refs):
    base = sum(counts)
    q_ref, k_ref, v_ref = refs[:3]
    outs, semaphores = refs[3:-1], refs[-1]
    copies = [
        pltpu.make_async_copy(source, target, semaphores.at[index])
        for index, (source, target) in enumerate(
            ((q_hbm, q_ref), (k_hbm, k_ref), (v_hbm, v_ref))
        )
    ]
    for copy in copies:
        copy.start()
    for copy in copies:
        copy.wait()
    columns = [head_columns(head) for head in range(base + keys_moved)]
    moving = [(ref, part) for ref in (k_ref, v_ref) for part in columns[base:]]
    start = 0
    up = place_ref[4] == 1

    def fill(out, parts):
        for index, (ref, part) in enumerate(parts):
            out[:, head_columns(index)] = ref[:, part]

    for i, count in enumerate(counts):
        cross_out, forward_out, backward_out = outs[3 * i : 3 * i + 3]
        own = columns[start : start + count]
        queries = [(q_ref, part) for part in own]
        keys = moving[start : start + count]
        crossing = [(ref, part) for ref in (k_ref, v_ref) for part in own]

        @pl.when(up)
        def _():
            fill(forward_out, keys)
            fill(backward_out, queries)

        @pl.when(jnp.logical_not(up))
        def _():
            fill(forward_out, queries)
            fill(backward_out, keys)

        fill(cross_out, crossing)
        if i == 0:

            @pl.when(place_ref[0] > 0)
            def _():
                fill(cross_out, [(q_ref, part) for part in columns[base:]])

        start += count


def crossing_keys(own_k, own_v, prior_kv, base, head, head_count):
    own_columns = head_columns(base + head)
    keys = jnp.concatenate([own_k[:, own_columns], prior_kv[:, head_columns(head)]], axis=0)
    values = jnp.concatenate(
        [own_v[:, own_columns], prior_kv[:, head_columns(head_count + head)]], axis=0
    )
    return keys, jnp.transpose(values)


def crossing_flags(place_ref, ranges_ref, distance, slot, pair_count):
    group, position = place_ref[0], place_ref[1]
    return [
        shown(
            place_ref,
            ranges_ref,
            group * pair_count + slot,
            position + distance,
            (group - behind) * pair_count + key_slot,
            position,
        )
        for behind in range(2)
        for key_slot in range(pair_count)
    ]


def far_kernel(
    head_count, place_ref, ranges_ref, own_k, own_v, forward_q, backward_q, prior_kv, *rest,
    base, pair_count,
):
    far_payload, far_stats = rest[-2:]
    up = place_ref[4] == 1
    seen = [crossing_flags(place_ref, ranges_ref, 2, slot, pair_count) for slot in range(pair_count)]
    stats = [jnp.zeros((1, BLOCK), jnp.float32)] * STAT_ROWS
    for head in range(head_count):
        columns = head_columns(head)
        keys, values = crossing_keys(own_k, own_v, prior_kv, base, head, head_count)
        for slot in range(pair_count):
            rows = stretch_rows(slot)
            query = pick(up, (backward_q, forward_q), rows, columns)
            attended, stats[slot * head_count + head] = attend(query, keys, values, seen[slot])
            far_payload[rows, columns] = attended.astype(jnp.bfloat16)
    far_stats[...] = jnp.concatenate(stats, axis=0)
    put_stats(far_payload, far_stats[...], pair_count * BLOCK)


def near_kernel(
    head_count, place_ref, ranges_ref, own_q, own_k, own_v, forward_q, backward_q, prior_kv,
    *rest, base, pair_count,
):
    own_out, own_stats, near_out, near_stats = rest[-4:]
    up = place_ref[4] == 1
    seen = {
        (distance, slot): crossing_flags(place_ref, ranges_ref, distance, slot, pair_count)
        for distance in range(2)
        for slot in range(pair_count)
    }
    own_stats[...] = jnp.zeros_like(own_stats)
    near_stats[...] = jnp.zeros_like(near_stats)
    for head in range(head_count):
        columns = head_columns(head)
        keys, values = crossing_keys(own_k, own_v, prior_kv, base, head, head_count)
        for slot in range(pair_count):
            rows = stretch_rows(slot)
            index = slot * head_count + head
            query = pick(up, (backward_q, forward_q), rows, columns)
            near_out[rows, columns], near_stats[index : index + 1, :] = attend(
                query, keys, values, seen[1, slot]
            )
            query = own_q[rows, head_columns(base + head)]
            own_out[rows, columns], own_stats[index : index + 1, :] = attend(
                query, keys, values, seen[0, slot]
            )


def keys_moved_kernel(
    head_count, place_ref, ranges_ref, own_q, own_k, own_v, next_q, *rest, base, pair_count, counts
):
    own_out, own_stats, next_payload = rest[-3:]
    group, position = place_ref[0], place_ref[1]
    up = place_ref[4] == 1
    parts = len(counts)
    came = [
        [rest[2 * (hop * parts + part) : 2 * (hop * parts + part) + 2] for part in range(parts)]
        for hop in range(REACH)
    ]

    def moved_block(hop, unit):
        part = 0
        while unit >= counts[part]:
            unit -= counts[part]
            part += 1
        return pick(up, came[hop][part], slice(None), head_columns(unit))

    seen = {
        (ahead, slot): [
            shown(
                place_ref,
                ranges_ref,
                (group + ahead) * pair_count + slot,
                position,
                group * pair_count + key_slot,
                position - distance,
            )
            for distance in range(REACH + 1)
            for key_slot in range(pair_count)
        ]
        for ahead in range(2)
        for slot in range(pair_count)
    }
    own_stats[...] = jnp.zeros_like(own_stats)
    next_stats = [jnp.zeros((1, BLOCK), jnp.float32)] * STAT_ROWS
    for head in range(head_count):
        columns, own_columns = head_columns(head), head_columns(base + head)
        keys = jnp.concatenate(
            [own_k[:, own_columns]] + [moved_block(hop, head) for hop in range(REACH)], axis=0
        )
        values = jnp.transpose(
            jnp.concatenate(
                [own_v[:, own_columns]]
                + [moved_block(hop, head_count + head) for hop in range(REACH)],
                axis=0,
            )
        )
        for slot in range(pair_count):
            rows = stretch_rows(slot)
            index = slot * head_count + head
            attended, next_stats[index] = attend(
                next_q[rows, columns], keys, values, seen[1, slot]
            )
            next_payload[rows, columns] = attended.astype(jnp.bfloat16)
            own_out[rows, columns], own_stats[index : index + 1, :] = attend(
                own_q[rows, own_columns], keys, values, seen[0, slot]
            )
    put_stats(next_payload, jnp.concatenate(next_stats, axis=0), pair_count * BLOCK)


def joined(sender_index, local_out, local_stats, payload_ref, head_count):
    token_rows = local_out.shape[0]
    local_log = local_stats[...]
    remote_log = jnp.where(sender_index > 0, get_stats(payload_ref, token_rows), HIDDEN)
    top = jnp.maximum(local_log, remote_log)
    local_weight = jnp.exp2(local_log - top)
    remote_weight = jnp.exp2(remote_log - top)
    both = local_weight + remote_weight
    scale = 1.0 / both
    local_weight = local_weight * scale
    remote_weight = remote_weight * scale
    parts = {}
    for slot in range(token_rows // BLOCK):
        for head in range(head_count):
            index = slot * head_count + head
            rows, columns = stretch_rows(slot), head_columns(head)
            parts[slot, head] = (
                local_out[rows, columns] * local_weight[index : index + 1]
                + payload_ref[rows, columns].astype(jnp.float32)
                * remote_weight[index : index + 1]
            )
    return parts, top + jnp.log2(both)


def relay_kernel(
    head_count, place_ref, local_out, local_stats, payload_in, *rest, axis
):
    payload_out, stats_out = rest[-2:]
    parts, log_total = joined(place_ref[axis], local_out, local_stats, payload_in, head_count)
    for (slot, head), part in parts.items():
        payload_out[stretch_rows(slot), head_columns(head)] = part.astype(jnp.bfloat16)
    stats_out[...] = log_total
    put_stats(payload_out, log_total, local_out.shape[0])


def finish_kernel(
    head_count, place_ref, local_out, local_stats, payload_in, squares_in, *rest, axis
):
    out, squares_out = rest[-2:]
    parts, _ = joined(place_ref[axis], local_out, local_stats, payload_in, head_count)
    squares_out[...] = squares_in[...]
    for slot in range(local_out.shape[0] // BLOCK):
        total = jnp.zeros((1, BLOCK), jnp.float32)
        for head in range(head_count):
            part = parts[slot, head]
            total = total + jnp.sum(part * part, axis=0, keepdims=True)
            out[stretch_rows(slot), head_columns(head)] = jnp.transpose(part)
        squares_out[slot : slot + 1, :] += total


def scale_kernel(head_counts, feature_count, place_ref, levels_ref, squares, gate_table, *refs):
    parts, out = refs[:-1], refs[-1]
    factors = as_columns(lax.rsqrt(squares[...] / feature_count + 1e-06))
    pair_count = out.shape[0] // BLOCK
    gates = gate_table[...].astype(jnp.float32)
    level_ids = lax.broadcasted_iota(jnp.int32, gates.shape, 0)
    for slot in range(pair_count):
        level = levels_ref[place_ref[0] * pair_count + slot]
        gate_row = jnp.sum(jnp.where(level_ids == level, gates, 0.0), axis=0, keepdims=True)
        rows = stretch_rows(slot)
        factor = factors[:, slot : slot + 1]
        base = 0
        for part, head_count in zip(parts, head_counts):
            for head in range(head_count):
                columns = head_columns(base + head)
                out[rows, columns] = (
                    part[rows, head_columns(head)] * factor * gate_row[:, columns]
                ).astype(jnp.bfloat16)
            base += head_count


def cost(microseconds):
    return pl.CostEstimate(
        flops=int(microseconds * 1e9), bytes_accessed=int(microseconds * 1e6), transcendentals=0
    )


SMEM = pl.BlockSpec(memory_space=pltpu.SMEM)
VMEM = pl.BlockSpec(memory_space=pltpu.VMEM)
PARAMS = pltpu.CompilerParams(vmem_limit_bytes=32 * 1024 * 1024)


def on_device(query_rows, key_rows, value_rows, gate_table, levels, kv_ranges):
    pair_count, row_count, width_dev = query_rows.shape
    assert row_count == BLOCK
    token_rows = pair_count * row_count
    head_total = width_dev // HEAD_DIM
    place = jnp.stack(
        [
            lax.axis_index("stretch"),
            lax.axis_index("cp"),
            jnp.int32(kv_ranges.shape[1]),
            jnp.int32(kv_ranges.shape[2]),
            goes_up(),
        ]
    ).astype(jnp.int32)
    queries, keys, values = (
        array.reshape(token_rows, width_dev) for array in (query_rows, key_rows, value_rows)
    )
    head_counts = CHUNKS + (KEYS_MOVED,)
    assert sum(head_counts) == head_total and 2 * KEYS_MOVED == sum(CHUNKS)
    assert lax.axis_size("stretch") == 2
    bases = [sum(head_counts[:i]) for i in range(len(head_counts))]
    widths = [count * HEAD_DIM for count in head_counts]
    chunks = range(len(CHUNKS))
    last = len(CHUNKS)

    def float_shape(chunk):
        return jax.ShapeDtypeStruct((token_rows, widths[chunk]), jnp.float32)

    def payload_shape(chunk):
        return jax.ShapeDtypeStruct((token_rows + STAT_ROWS, widths[chunk]), jnp.bfloat16)

    stats_shape = jax.ShapeDtypeStruct((STAT_ROWS, BLOCK), jnp.float32)
    squares_shape = jax.ShapeDtypeStruct((8, BLOCK), jnp.float32)

    def run(name, kernel, chunk, microseconds, out_shape, smem, vmem, after=()):
        return pl.pallas_call(
            functools.partial(kernel, head_counts[chunk]),
            out_shape=out_shape,
            in_specs=[SMEM] * len(smem)
            + [VMEM] * len(vmem)
            + [pl.BlockSpec(memory_space=pl.ANY)] * len(after),
            out_specs=(VMEM,) * len(out_shape),
            compiler_params=PARAMS,
            cost_estimate=cost(microseconds),
            name=name,
        )(*smem, *vmem, *after)

    def block_shape(units):
        return jax.ShapeDtypeStruct((token_rows, units * HEAD_DIM), jnp.bfloat16)

    packed = pl.pallas_call(
        functools.partial(pack_kernel, CHUNKS, KEYS_MOVED),
        out_shape=(block_shape(head_total),) * 3
        + tuple(block_shape(units) for count in CHUNKS for units in (2 * count, count, count)),
        in_specs=[SMEM] + [pl.BlockSpec(memory_space=pltpu.HBM)] * 3,
        out_specs=(VMEM,) * (3 + 3 * len(CHUNKS)),
        scratch_shapes=[pltpu.SemaphoreType.DMA((3,))],
        compiler_params=pltpu.CompilerParams(vmem_limit_bytes=PACK_LIMIT),
        cost_estimate=cost(1.0),
        name="pack",
    )(place, queries, keys, values)
    queries, keys, values = packed[:3]
    prior_kv, hops = [], [[], []]
    for i in chunks:
        crossing, forward, backward = packed[3 * i + 3 : 3 * i + 6]
        prior_kv.append(exchanged(crossing))
        hops[0].append((round_trip(forward, True), round_trip(backward, False)))
    for i in chunks:
        forward, backward = hops[0][i]
        hops[1].append((round_trip(forward, True), round_trip(backward, False)))

    own_parts, near_parts, arrived = [], [], []
    turn = ()
    for i in chunks:
        near = run(
            "near",
            functools.partial(near_kernel, base=bases[i], pair_count=pair_count),
            i,
            NEAR_COST[i],
            (float_shape(i), stats_shape) * 2,
            (place, kv_ranges),
            (queries, keys, values, *hops[0][i], prior_kv[i]),
            turn,
        )
        own_parts.append(near[:2])
        near_parts.append(near[2:])
        far_payload, far_stats = run(
            "far",
            functools.partial(far_kernel, base=bases[i], pair_count=pair_count),
            i,
            FAR_COST[i],
            (payload_shape(i), stats_shape),
            (place, kv_ranges),
            (keys, values, *hops[1][i], prior_kv[i]),
            (near[1],),
        )
        turn = (far_stats,)
        arrived.append(passed_up(far_payload))
    own_out, own_stats, next_payload = run(
        "keys_moved",
        functools.partial(
            keys_moved_kernel, base=bases[last], pair_count=pair_count, counts=CHUNKS
        ),
        last,
        KEYS_COST,
        (float_shape(last), stats_shape, payload_shape(last)),
        (place, kv_ranges),
        (queries, keys, values, prior_kv[0], *[ref for hop in hops for pair in hop for ref in pair]),
        turn,
    )
    own_parts.append((own_out, own_stats))
    turn = (own_stats,)
    arrived.append(exchanged(next_payload))
    for i in chunks:
        relayed, relayed_stats = run(
            "relay",
            functools.partial(relay_kernel, axis=1),
            i,
            0.7,
            (payload_shape(i), stats_shape),
            (place,),
            (*near_parts[i], arrived[i]),
            turn,
        )
        turn = (relayed_stats,)
        arrived[i] = passed_up(relayed)
    squares = jnp.zeros(squares_shape.shape, jnp.float32)
    finished = [None] * len(head_counts)
    for i in FINISH_ORDER:
        finished[i], squares = run(
            "finish",
            functools.partial(finish_kernel, axis=0 if i == last else 1),
            i,
            0.8,
            (float_shape(i), squares_shape),
            (place,),
            (*own_parts[i], arrived[i], squares),
            turn,
        )
    squares = lax.psum(squares, "tp")
    out = pl.pallas_call(
        functools.partial(scale_kernel, head_counts, float(HEADS * HEAD_DIM)),
        out_shape=jax.ShapeDtypeStruct((token_rows, width_dev), jnp.bfloat16),
        in_specs=[SMEM, SMEM] + [VMEM] * (2 + len(finished)),
        out_specs=VMEM,
        compiler_params=PARAMS,
    )(place, levels, squares, gate_table, *finished)
    return out.reshape(query_rows.shape)


def solution(mesh):
    in_specs = (
        P("stretch", "cp", "tp"),
        P("stretch", "cp", "tp"),
        P("stretch", "cp", "tp"),
        P(None, "tp"),
        P(),
        P(),
    )
    out_specs = P("stretch", "cp", "tp")
    return jax.shard_map(
        on_device, mesh=mesh, in_specs=in_specs, out_specs=out_specs, check_vma=False
    )
```

```python
import functools
import math

import jax
import jax.numpy as jnp
from jax import lax
from jax.experimental import pallas as pl
from jax.experimental.pallas import tpu as pltpu
from jax.sharding import PartitionSpec as P

HEADS = 48
HEAD_DIM = 128
BLOCK = 128
REACH = 2
CHUNKS = (5, 3)
KEYS_MOVED = 4
FINISH_ORDER = (2, 0, 1)
WRAP = True
NEAR_COST = (3.0, 1.8)
FAR_COST = (1.5, 0.9)
KEYS_COST = 2.0
PACK_LIMIT = 49 * 1024 * 1024
STAT_ROWS = 16
HIDDEN = -1e30
EXPONENT_SCALE = math.log2(math.e) / math.sqrt(HEAD_DIM)


def exchanged(block):
    return lax.ppermute(block, "stretch", [(0, 1), (1, 0)])


def goes_up():
    return lax.axis_index("tp") < lax.axis_size("tp") // 2


def round_trip(block, forward):
    count, half = lax.axis_size("cp"), lax.axis_size("tp") // 2
    route = []
    for lane in range(half):
        cycle = [i * 2 * half + lane for i in range(count)]
        cycle += [i * 2 * half + half + lane for i in reversed(range(count))]
        route += zip(cycle, cycle[1:] + cycle[:1])
    if not forward:
        route = [(target, source) for source, target in route]
    return lax.ppermute(block, ("cp", "tp"), route)


def passed_up(block):
    count = lax.axis_size("cp")
    route = [(i, (i + 1) % count) for i in range(count if WRAP else count - 1)]
    return lax.ppermute(block, "cp", route)


def head_columns(head):
    return slice(head * HEAD_DIM, (head + 1) * HEAD_DIM)


def stretch_rows(slot):
    return slice(slot * BLOCK, (slot + 1) * BLOCK)


def as_columns(rows):
    fill = jnp.zeros((BLOCK - rows.shape[0], BLOCK), jnp.float32)
    return jnp.transpose(jnp.concatenate([rows, fill], axis=0))


def put_stats(payload_ref, stats, token_rows):
    high = stats.astype(jnp.bfloat16)
    rest = stats - high.astype(jnp.float32)
    middle = rest.astype(jnp.bfloat16)
    low = (rest - middle.astype(jnp.float32)).astype(jnp.bfloat16)
    rows = slice(token_rows, token_rows + STAT_ROWS)
    for index, piece in enumerate((high, middle, low)):
        payload_ref[rows, head_columns(index)] = piece


def get_stats(payload_ref, token_rows):
    rows = slice(token_rows, token_rows + STAT_ROWS)
    pieces = [
        payload_ref[rows, head_columns(index)].astype(jnp.float32) for index in range(3)
    ]
    return (pieces[0] + pieces[1]) + pieces[2]


def shown(place_ref, ranges_ref, query_stretch, query_block, key_stretch, key_block):
    stretch_count, block_count = place_ref[2], place_ref[3]
    low, high = (
        ranges_ref[
            end,
            jnp.minimum(query_stretch, stretch_count - 1),
            jnp.minimum(query_block, block_count - 1),
            jnp.maximum(key_stretch, 0),
        ]
        for end in range(2)
    )
    exists = (
        (query_stretch < stretch_count)
        & (query_block < block_count)
        & (key_stretch >= 0)
        & (key_block >= 0)
    )
    return exists & (low <= key_block) & (key_block < high)


def attend(query, keys, values, seen):
    scores = lax.dot_general(
        keys, query, (((1,), (1,)), ((), ())), preferred_element_type=jnp.float32
    )
    blocks = [scores[stretch_rows(j)] for j in range(len(seen))]
    peak = jnp.full((1, BLOCK), HIDDEN, jnp.float32)
    for block, flag in zip(blocks, seen):
        block_peak = jnp.max(block, axis=0, keepdims=True)
        peak = jnp.maximum(peak, jnp.where(flag, block_peak, HIDDEN))
    shift = peak * EXPONENT_SCALE
    weights = [
        jnp.exp2(block * EXPONENT_SCALE - jnp.where(flag, shift, -HIDDEN))
        for block, flag in zip(blocks, seen)
    ]
    total = sum(jnp.sum(weight, axis=0, keepdims=True) for weight in weights)
    weights = jnp.concatenate([weight.astype(jnp.bfloat16) for weight in weights], axis=0)
    summed = jnp.dot(values, weights, preferred_element_type=jnp.float32)
    total = jnp.maximum(total, 1e-30)
    return summed * (1.0 / total), jnp.maximum(shift + jnp.log2(total), HIDDEN)


def pick(up, refs, *index):
    return jnp.where(up, refs[0][index], refs[1][index])


def pack_kernel(counts, keys_moved, place_ref, q_hbm, k_hbm, v_hbm, *refs):
    base = sum(counts)
    q_ref, k_ref, v_ref = refs[:3]
    outs, semaphores = refs[3:-1], refs[-1]
    copies = [
        pltpu.make_async_copy(source, target, semaphores.at[index])
        for index, (source, target) in enumerate(
            ((q_hbm, q_ref), (k_hbm, k_ref), (v_hbm, v_ref))
        )
    ]
    for copy in copies:
        copy.start()
    for copy in copies:
        copy.wait()
    columns = [head_columns(head) for head in range(base + keys_moved)]
    moving = [(ref, part) for ref in (k_ref, v_ref) for part in columns[base:]]
    start = 0
    up = place_ref[4] == 1

    def fill(out, parts):
        for index, (ref, part) in enumerate(parts):
            out[:, head_columns(index)] = ref[:, part]

    for i, count in enumerate(counts):
        cross_out, forward_out, backward_out = outs[3 * i : 3 * i + 3]
        own = columns[start : start + count]
        queries = [(q_ref, part) for part in own]
        keys = moving[start : start + count]
        crossing = [(ref, part) for ref in (k_ref, v_ref) for part in own]

        @pl.when(up)
        def _():
            fill(forward_out, keys)
            fill(backward_out, queries)

        @pl.when(jnp.logical_not(up))
        def _():
            fill(forward_out, queries)
            fill(backward_out, keys)

        fill(cross_out, crossing)
        if i == 0:

            @pl.when(place_ref[0] > 0)
            def _():
                fill(cross_out, [(q_ref, part) for part in columns[base:]])

        start += count


def crossing_keys(own_k, own_v, prior_kv, base, head, head_count):
    own_columns = head_columns(base + head)
    keys = jnp.concatenate([own_k[:, own_columns], prior_kv[:, head_columns(head)]], axis=0)
    values = jnp.concatenate(
        [own_v[:, own_columns], prior_kv[:, head_columns(head_count + head)]], axis=0
    )
    return keys, jnp.transpose(values)


def crossing_flags(place_ref, ranges_ref, distance, slot, pair_count):
    group, position = place_ref[0], place_ref[1]
    return [
        shown(
            place_ref,
            ranges_ref,
            group * pair_count + slot,
            position + distance,
            (group - behind) * pair_count + key_slot,
            position,
        )
        for behind in range(2)
        for key_slot in range(pair_count)
    ]


def far_kernel(
    head_count, place_ref, ranges_ref, own_k, own_v, forward_q, backward_q, prior_kv, *rest,
    base, pair_count,
):
    far_payload, far_stats = rest[-2:]
    up = place_ref[4] == 1
    seen = [crossing_flags(place_ref, ranges_ref, 2, slot, pair_count) for slot in range(pair_count)]
    stats = [jnp.zeros((1, BLOCK), jnp.float32)] * STAT_ROWS
    for head in range(head_count):
        columns = head_columns(head)
        keys, values = crossing_keys(own_k, own_v, prior_kv, base, head, head_count)
        for slot in range(pair_count):
            rows = stretch_rows(slot)
            query = pick(up, (backward_q, forward_q), rows, columns)
            attended, stats[slot * head_count + head] = attend(query, keys, values, seen[slot])
            far_payload[rows, columns] = attended.astype(jnp.bfloat16)
    far_stats[...] = jnp.concatenate(stats, axis=0)
    put_stats(far_payload, far_stats[...], pair_count * BLOCK)


def near_kernel(
    head_count, place_ref, ranges_ref, own_q, own_k, own_v, forward_q, backward_q, prior_kv,
    *rest, base, pair_count,
):
    own_out, own_stats, near_out, near_stats = rest[-4:]
    up = place_ref[4] == 1
    seen = {
        (distance, slot): crossing_flags(place_ref, ranges_ref, distance, slot, pair_count)
        for distance in range(2)
        for slot in range(pair_count)
    }
    own_stats[...] = jnp.zeros_like(own_stats)
    near_stats[...] = jnp.zeros_like(near_stats)
    for head in range(head_count):
        columns = head_columns(head)
        keys, values = crossing_keys(own_k, own_v, prior_kv, base, head, head_count)
        for slot in range(pair_count):
            rows = stretch_rows(slot)
            index = slot * head_count + head
            query = pick(up, (backward_q, forward_q), rows, columns)
            near_out[rows, columns], near_stats[index : index + 1, :] = attend(
                query, keys, values, seen[1, slot]
            )
            query = own_q[rows, head_columns(base + head)]
            own_out[rows, columns], own_stats[index : index + 1, :] = attend(
                query, keys, values, seen[0, slot]
            )


def keys_moved_kernel(
    head_count, place_ref, ranges_ref, own_q, own_k, own_v, next_q, *rest, base, pair_count, counts
):
    own_out, own_stats, next_payload = rest[-3:]
    group, position = place_ref[0], place_ref[1]
    up = place_ref[4] == 1
    parts = len(counts)
    came = [
        [rest[2 * (hop * parts + part) : 2 * (hop * parts + part) + 2] for part in range(parts)]
        for hop in range(REACH)
    ]

    def moved_block(hop, unit):
        part = 0
        while unit >= counts[part]:
            unit -= counts[part]
            part += 1
        return pick(up, came[hop][part], slice(None), head_columns(unit))

    seen = {
        (ahead, slot): [
            shown(
                place_ref,
                ranges_ref,
                (group + ahead) * pair_count + slot,
                position,
                group * pair_count + key_slot,
                position - distance,
            )
            for distance in range(REACH + 1)
            for key_slot in range(pair_count)
        ]
        for ahead in range(2)
        for slot in range(pair_count)
    }
    own_stats[...] = jnp.zeros_like(own_stats)
    next_stats = [jnp.zeros((1, BLOCK), jnp.float32)] * STAT_ROWS
    for head in range(head_count):
        columns, own_columns = head_columns(head), head_columns(base + head)
        keys = jnp.concatenate(
            [own_k[:, own_columns]] + [moved_block(hop, head) for hop in range(REACH)], axis=0
        )
        values = jnp.transpose(
            jnp.concatenate(
                [own_v[:, own_columns]]
                + [moved_block(hop, head_count + head) for hop in range(REACH)],
                axis=0,
            )
        )
        for slot in range(pair_count):
            rows = stretch_rows(slot)
            index = slot * head_count + head
            attended, next_stats[index] = attend(
                next_q[rows, columns], keys, values, seen[1, slot]
            )
            next_payload[rows, columns] = attended.astype(jnp.bfloat16)
            own_out[rows, columns], own_stats[index : index + 1, :] = attend(
                own_q[rows, own_columns], keys, values, seen[0, slot]
            )
    put_stats(next_payload, jnp.concatenate(next_stats, axis=0), pair_count * BLOCK)


def joined(sender_index, local_out, local_stats, payload_ref, head_count):
    token_rows = local_out.shape[0]
    local_log = local_stats[...]
    remote_log = jnp.where(sender_index > 0, get_stats(payload_ref, token_rows), HIDDEN)
    top = jnp.maximum(local_log, remote_log)
    local_weight = jnp.exp2(local_log - top)
    remote_weight = jnp.exp2(remote_log - top)
    both = local_weight + remote_weight
    scale = 1.0 / both
    local_weight = local_weight * scale
    remote_weight = remote_weight * scale
    parts = {}
    for slot in range(token_rows // BLOCK):
        for head in range(head_count):
            index = slot * head_count + head
            rows, columns = stretch_rows(slot), head_columns(head)
            parts[slot, head] = (
                local_out[rows, columns] * local_weight[index : index + 1]
                + payload_ref[rows, columns].astype(jnp.float32)
                * remote_weight[index : index + 1]
            )
    return parts, top + jnp.log2(both)


def relay_kernel(
    head_count, place_ref, local_out, local_stats, payload_in, *rest, axis
):
    payload_out, stats_out = rest[-2:]
    parts, log_total = joined(place_ref[axis], local_out, local_stats, payload_in, head_count)
    for (slot, head), part in parts.items():
        payload_out[stretch_rows(slot), head_columns(head)] = part.astype(jnp.bfloat16)
    stats_out[...] = log_total
    put_stats(payload_out, log_total, local_out.shape[0])


def finish_kernel(
    head_count, place_ref, local_out, local_stats, payload_in, gates, squares_in, *rest, axis, base
):
    out, squares_out = rest[-2:]
    parts, _ = joined(place_ref[axis], local_out, local_stats, payload_in, head_count)
    squares_out[...] = squares_in[...]
    for slot in range(local_out.shape[0] // BLOCK):
        total = jnp.zeros((1, BLOCK), jnp.float32)
        for head in range(head_count):
            part = parts[slot, head]
            total = total + jnp.sum(part * part, axis=0, keepdims=True)
            gate_row = gates[slot : slot + 1, head_columns(base + head)]
            out[stretch_rows(slot), head_columns(head)] = jnp.transpose(part) * gate_row
        squares_out[slot : slot + 1, :] += total


def gates_kernel(pair_count, place_ref, levels_ref, gate_table, *rest):
    out = rest[-1]
    gates = gate_table[...].astype(jnp.float32)
    level_ids = lax.broadcasted_iota(jnp.int32, gates.shape, 0)
    out[...] = jnp.zeros_like(out)
    for slot in range(pair_count):
        level = levels_ref[place_ref[0] * pair_count + slot]
        out[slot : slot + 1, :] = jnp.sum(
            jnp.where(level_ids == level, gates, 0.0), axis=0, keepdims=True
        )


def scale_kernel(head_counts, feature_count, device_count, *refs):
    squares = sum(ref[...] for ref in refs[:device_count])
    parts, out = refs[device_count:-1], refs[-1]
    factors = as_columns(lax.rsqrt(squares / feature_count + 1e-06))
    for slot in range(out.shape[0] // BLOCK):
        rows = stretch_rows(slot)
        factor = factors[:, slot : slot + 1]
        base = 0
        for part, head_count in zip(parts, head_counts):
            for head in range(head_count):
                out[rows, head_columns(base + head)] = (
                    part[rows, head_columns(head)] * factor
                ).astype(jnp.bfloat16)
            base += head_count


def cost(microseconds):
    return pl.CostEstimate(
        flops=int(microseconds * 1e9), bytes_accessed=int(microseconds * 1e6), transcendentals=0
    )


SMEM = pl.BlockSpec(memory_space=pltpu.SMEM)
VMEM = pl.BlockSpec(memory_space=pltpu.VMEM)
PARAMS = pltpu.CompilerParams(vmem_limit_bytes=32 * 1024 * 1024)


def on_device(query_rows, key_rows, value_rows, gate_table, levels, kv_ranges):
    pair_count, row_count, width_dev = query_rows.shape
    assert row_count == BLOCK
    token_rows = pair_count * row_count
    head_total = width_dev // HEAD_DIM
    place = jnp.stack(
        [
            lax.axis_index("stretch"),
            lax.axis_index("cp"),
            jnp.int32(kv_ranges.shape[1]),
            jnp.int32(kv_ranges.shape[2]),
            goes_up(),
        ]
    ).astype(jnp.int32)
    queries, keys, values = (
        array.reshape(token_rows, width_dev) for array in (query_rows, key_rows, value_rows)
    )
    head_counts = CHUNKS + (KEYS_MOVED,)
    assert sum(head_counts) == head_total and 2 * KEYS_MOVED == sum(CHUNKS)
    assert lax.axis_size("stretch") == 2
    bases = [sum(head_counts[:i]) for i in range(len(head_counts))]
    widths = [count * HEAD_DIM for count in head_counts]
    chunks = range(len(CHUNKS))
    last = len(CHUNKS)

    def float_shape(chunk):
        return jax.ShapeDtypeStruct((token_rows, widths[chunk]), jnp.float32)

    def payload_shape(chunk):
        return jax.ShapeDtypeStruct((token_rows + STAT_ROWS, widths[chunk]), jnp.bfloat16)

    stats_shape = jax.ShapeDtypeStruct((STAT_ROWS, BLOCK), jnp.float32)
    squares_shape = jax.ShapeDtypeStruct((8, BLOCK), jnp.float32)

    def run(name, kernel, chunk, microseconds, out_shape, smem, vmem, after=()):
        return pl.pallas_call(
            functools.partial(kernel, head_counts[chunk]),
            out_shape=out_shape,
            in_specs=[SMEM] * len(smem)
            + [VMEM] * len(vmem)
            + [pl.BlockSpec(memory_space=pl.ANY)] * len(after),
            out_specs=(VMEM,) * len(out_shape),
            compiler_params=PARAMS,
            cost_estimate=cost(microseconds),
            name=name,
        )(*smem, *vmem, *after)

    def block_shape(units):
        return jax.ShapeDtypeStruct((token_rows, units * HEAD_DIM), jnp.bfloat16)

    packed = pl.pallas_call(
        functools.partial(pack_kernel, CHUNKS, KEYS_MOVED),
        out_shape=(block_shape(head_total),) * 3
        + tuple(block_shape(units) for count in CHUNKS for units in (2 * count, count, count)),
        in_specs=[SMEM] + [pl.BlockSpec(memory_space=pltpu.HBM)] * 3,
        out_specs=(VMEM,) * (3 + 3 * len(CHUNKS)),
        scratch_shapes=[pltpu.SemaphoreType.DMA((3,))],
        compiler_params=pltpu.CompilerParams(vmem_limit_bytes=PACK_LIMIT),
        cost_estimate=cost(1.0),
        name="pack",
    )(place, queries, keys, values)
    queries, keys, values = packed[:3]
    prior_kv, hops = [], [[], []]
    for i in chunks:
        crossing, forward, backward = packed[3 * i + 3 : 3 * i + 6]
        prior_kv.append(exchanged(crossing))
        hops[0].append((round_trip(forward, True), round_trip(backward, False)))
    for i in chunks:
        forward, backward = hops[0][i]
        hops[1].append((round_trip(forward, True), round_trip(backward, False)))

    own_parts, near_parts, arrived = [], [], []
    gates = pl.pallas_call(
        functools.partial(gates_kernel, pair_count),
        out_shape=jax.ShapeDtypeStruct((8, width_dev), jnp.float32),
        in_specs=[SMEM, SMEM, VMEM],
        out_specs=VMEM,
        compiler_params=PARAMS,
        cost_estimate=cost(0.6),
        name="gates",
    )(place, levels, gate_table)
    turn = (gates,)
    for i in chunks:
        near = run(
            "near",
            functools.partial(near_kernel, base=bases[i], pair_count=pair_count),
            i,
            NEAR_COST[i],
            (float_shape(i), stats_shape) * 2,
            (place, kv_ranges),
            (queries, keys, values, *hops[0][i], prior_kv[i]),
            turn,
        )
        own_parts.append(near[:2])
        near_parts.append(near[2:])
        far_payload, far_stats = run(
            "far",
            functools.partial(far_kernel, base=bases[i], pair_count=pair_count),
            i,
            FAR_COST[i],
            (payload_shape(i), stats_shape),
            (place, kv_ranges),
            (keys, values, *hops[1][i], prior_kv[i]),
            (near[1],),
        )
        turn = (far_stats,)
        arrived.append(passed_up(far_payload))
    own_out, own_stats, next_payload = run(
        "keys_moved",
        functools.partial(
            keys_moved_kernel, base=bases[last], pair_count=pair_count, counts=CHUNKS
        ),
        last,
        KEYS_COST,
        (float_shape(last), stats_shape, payload_shape(last)),
        (place, kv_ranges),
        (queries, keys, values, prior_kv[0], *[ref for hop in hops for pair in hop for ref in pair]),
        turn,
    )
    own_parts.append((own_out, own_stats))
    turn = (own_stats,)
    arrived.append(exchanged(next_payload))
    for i in chunks:
        relayed, relayed_stats = run(
            "relay",
            functools.partial(relay_kernel, axis=1),
            i,
            0.7,
            (payload_shape(i), stats_shape),
            (place,),
            (*near_parts[i], arrived[i]),
            turn,
        )
        turn = (relayed_stats,)
        arrived[i] = passed_up(relayed)
    squares = jnp.zeros(squares_shape.shape, jnp.float32)
    finished = [None] * len(head_counts)
    for i in FINISH_ORDER:
        finished[i], squares = run(
            "finish",
            functools.partial(finish_kernel, axis=0 if i == last else 1, base=bases[i]),
            i,
            0.8,
            (float_shape(i), squares_shape),
            (place,),
            (*own_parts[i], arrived[i], gates, squares),
            turn,
        )
    device_count = lax.axis_size("tp")
    shares = [squares]
    for distance in range(1, device_count):
        route = [(i, (i + distance) % device_count) for i in range(device_count)]
        shares.append(lax.ppermute(squares, "tp", route))
    out = pl.pallas_call(
        functools.partial(scale_kernel, head_counts, float(HEADS * HEAD_DIM), device_count),
        out_shape=jax.ShapeDtypeStruct((token_rows, width_dev), jnp.bfloat16),
        in_specs=[VMEM] * (device_count + len(finished)),
        out_specs=VMEM,
        compiler_params=PARAMS,
        name="scale",
    )(*shares, *finished)
    return out.reshape(query_rows.shape)


def solution(mesh):
    in_specs = (
        P("stretch", "cp", "tp"),
        P("stretch", "cp", "tp"),
        P("stretch", "cp", "tp"),
        P(None, "tp"),
        P(),
        P(),
    )
    out_specs = P("stretch", "cp", "tp")
    return jax.shard_map(
        on_device, mesh=mesh, in_specs=in_specs, out_specs=out_specs, check_vma=False
    )
```

```python
import functools
import math

import jax
import jax.numpy as jnp
from jax import lax
from jax.experimental import pallas as pl
from jax.experimental.pallas import tpu as pltpu
from jax.sharding import PartitionSpec as P

HEADS = 48
HEAD_DIM = 128
BLOCK = 128
REACH = 2
CHUNKS = (5, 3)
KEYS_MOVED = 4
FINISH_ORDER = (2, 0, 1)
WRAP = True
NEAR_COST = (3.0, 1.8)
FAR_COST = (1.5, 0.9)
KEYS_COST = 2.0
PACK_LIMIT = 49 * 1024 * 1024
STAT_ROWS = 16
FLAGS = 64
HIDDEN = -1e30
EXPONENT_SCALE = math.log2(math.e) / math.sqrt(HEAD_DIM)


def exchanged(block):
    return lax.ppermute(block, "stretch", [(0, 1), (1, 0)])


def goes_up():
    return lax.axis_index("tp") < lax.axis_size("tp") // 2


def round_trip(block, forward):
    count, half = lax.axis_size("cp"), lax.axis_size("tp") // 2
    route = []
    for lane in range(half):
        cycle = [i * 2 * half + lane for i in range(count)]
        cycle += [i * 2 * half + half + lane for i in reversed(range(count))]
        route += zip(cycle, cycle[1:] + cycle[:1])
    if not forward:
        route = [(target, source) for source, target in route]
    return lax.ppermute(block, ("cp", "tp"), route)


def passed_up(block, wrap):
    count = lax.axis_size("cp")
    route = [(i, (i + 1) % count) for i in range(count if wrap else count - 1)]
    return lax.ppermute(block, "cp", route)


def head_columns(head):
    return slice(head * HEAD_DIM, (head + 1) * HEAD_DIM)


def stretch_rows(slot):
    return slice(slot * BLOCK, (slot + 1) * BLOCK)


def as_columns(rows):
    fill = jnp.zeros((BLOCK - rows.shape[0], BLOCK), jnp.float32)
    return jnp.transpose(jnp.concatenate([rows, fill], axis=0))


def put_stats(payload_ref, stats, token_rows):
    high = stats.astype(jnp.bfloat16)
    rest = stats - high.astype(jnp.float32)
    middle = rest.astype(jnp.bfloat16)
    low = (rest - middle.astype(jnp.float32)).astype(jnp.bfloat16)
    rows = slice(token_rows, token_rows + STAT_ROWS)
    for index, piece in enumerate((high, middle, low)):
        payload_ref[rows, head_columns(index)] = piece


def get_stats(payload_ref, token_rows):
    rows = slice(token_rows, token_rows + STAT_ROWS)
    pieces = [
        payload_ref[rows, head_columns(index)].astype(jnp.float32) for index in range(3)
    ]
    return (pieces[0] + pieces[1]) + pieces[2]


def shown(place_ref, ranges_ref, query_stretch, query_block, key_stretch, key_block):
    stretch_count, block_count = place_ref[2], place_ref[3]
    low, high = (
        ranges_ref[
            end,
            jnp.minimum(query_stretch, stretch_count - 1),
            jnp.minimum(query_block, block_count - 1),
            jnp.maximum(key_stretch, 0),
        ]
        for end in range(2)
    )
    exists = (
        (query_stretch < stretch_count)
        & (query_block < block_count)
        & (key_stretch >= 0)
        & (key_block >= 0)
    )
    return exists & (low <= key_block) & (key_block < high)


def attend(query, keys, values, seen):
    scores = lax.dot_general(
        keys, query, (((1,), (1,)), ((), ())), preferred_element_type=jnp.float32
    )
    blocks = [scores[stretch_rows(j)] for j in range(len(seen))]
    peak = jnp.full((1, BLOCK), HIDDEN, jnp.float32)
    for block, flag in zip(blocks, seen):
        block_peak = jnp.max(block, axis=0, keepdims=True)
        peak = jnp.maximum(peak, jnp.where(flag, block_peak, HIDDEN))
    shift = peak * EXPONENT_SCALE
    weights = [
        jnp.exp2(block * EXPONENT_SCALE - jnp.where(flag, shift, -HIDDEN))
        for block, flag in zip(blocks, seen)
    ]
    total = sum(jnp.sum(weight, axis=0, keepdims=True) for weight in weights)
    weights = jnp.concatenate([weight.astype(jnp.bfloat16) for weight in weights], axis=0)
    summed = jnp.dot(values, weights, preferred_element_type=jnp.float32)
    total = jnp.maximum(total, 1e-30)
    return summed * (1.0 / total), jnp.maximum(shift + jnp.log2(total), HIDDEN)


def pick(up, refs, *index):
    return jnp.where(up, refs[0][index], refs[1][index])


def pack_kernel(counts, keys_moved, place_ref, q_hbm, k_hbm, v_hbm, *refs):
    base = sum(counts)
    q_ref, k_ref, v_ref = refs[:3]
    outs, semaphores = refs[3:-1], refs[-1]
    copies = [
        pltpu.make_async_copy(source, target, semaphores.at[index])
        for index, (source, target) in enumerate(
            ((q_hbm, q_ref), (k_hbm, k_ref), (v_hbm, v_ref))
        )
    ]
    for copy in copies:
        copy.start()
    for copy in copies:
        copy.wait()
    columns = [head_columns(head) for head in range(base + keys_moved)]
    moving = [(ref, part) for ref in (k_ref, v_ref) for part in columns[base:]]
    start = 0
    up = place_ref[4] == 1

    def fill(out, parts):
        for index, (ref, part) in enumerate(parts):
            out[:, head_columns(index)] = ref[:, part]

    for i, count in enumerate(counts):
        cross_out, forward_out, backward_out = outs[3 * i : 3 * i + 3]
        own = columns[start : start + count]
        queries = [(q_ref, part) for part in own]
        keys = moving[start : start + count]
        crossing = [(ref, part) for ref in (k_ref, v_ref) for part in own]

        @pl.when(up)
        def _():
            fill(forward_out, keys)
            fill(backward_out, queries)

        @pl.when(jnp.logical_not(up))
        def _():
            fill(forward_out, queries)
            fill(backward_out, keys)

        fill(cross_out, crossing)
        if i == 0:

            @pl.when(place_ref[0] > 0)
            def _():
                fill(cross_out, [(q_ref, part) for part in columns[base:]])

        start += count


def crossing_keys(own_k, own_v, prior_kv, base, head, head_count):
    own_columns = head_columns(base + head)
    keys = jnp.concatenate([own_k[:, own_columns], prior_kv[:, head_columns(head)]], axis=0)
    values = jnp.concatenate(
        [own_v[:, own_columns], prior_kv[:, head_columns(head_count + head)]], axis=0
    )
    return keys, jnp.transpose(values)


def plan_kernel(pair_count, place_ref, ranges_ref, levels_ref, gate_table, *rest):
    gates_out, flags_out = rest[-2:]
    gates = gate_table[...].astype(jnp.float32)
    level_ids = lax.broadcasted_iota(jnp.int32, gates.shape, 0)
    gates_out[...] = jnp.zeros_like(gates_out)
    for slot in range(pair_count):
        level = levels_ref[place_ref[0] * pair_count + slot]
        gates_out[slot : slot + 1, :] = jnp.sum(
            jnp.where(level_ids == level, gates, 0.0), axis=0, keepdims=True
        )
    group, position = place_ref[0], place_ref[1]
    flags_out[0] = place_ref[4]
    index = 1
    for distance in range(REACH + 1):
        for slot in range(pair_count):
            for behind in range(2):
                for key_slot in range(pair_count):
                    flag = shown(
                        place_ref,
                        ranges_ref,
                        group * pair_count + slot,
                        position + distance,
                        (group - behind) * pair_count + key_slot,
                        position,
                    )
                    flags_out[index] = flag.astype(jnp.int32)
                    index += 1
    for ahead in range(2):
        for slot in range(pair_count):
            for distance in range(REACH + 1):
                for key_slot in range(pair_count):
                    flag = shown(
                        place_ref,
                        ranges_ref,
                        (group + ahead) * pair_count + slot,
                        position,
                        group * pair_count + key_slot,
                        position - distance,
                    )
                    flags_out[index] = flag.astype(jnp.int32)
                    index += 1


def crossing_flags(flags_ref, distance, slot, pair_count):
    base = 1 + (distance * pair_count + slot) * 2 * pair_count
    return [flags_ref[base + j] == 1 for j in range(2 * pair_count)]


def moved_flags(flags_ref, ahead, slot, pair_count):
    count = (REACH + 1) * pair_count
    base = 1 + count * 2 * pair_count + (ahead * pair_count + slot) * count
    return [flags_ref[base + j] == 1 for j in range(count)]


def far_kernel(
    head_count, flags_ref, own_k, own_v, forward_q, backward_q, prior_kv, *rest,
    base, pair_count,
):
    far_payload, far_stats = rest[-2:]
    up = flags_ref[0] == 1
    seen = [crossing_flags(flags_ref, 2, slot, pair_count) for slot in range(pair_count)]
    stats = [jnp.zeros((1, BLOCK), jnp.float32)] * STAT_ROWS
    for head in range(head_count):
        columns = head_columns(head)
        keys, values = crossing_keys(own_k, own_v, prior_kv, base, head, head_count)
        for slot in range(pair_count):
            rows = stretch_rows(slot)
            query = pick(up, (backward_q, forward_q), rows, columns)
            attended, stats[slot * head_count + head] = attend(query, keys, values, seen[slot])
            far_payload[rows, columns] = attended.astype(jnp.bfloat16)
    far_stats[...] = jnp.concatenate(stats, axis=0)
    put_stats(far_payload, far_stats[...], pair_count * BLOCK)


def near_kernel(
    head_count, flags_ref, own_q, own_k, own_v, forward_q, backward_q, prior_kv,
    *rest, base, pair_count,
):
    own_out, own_stats, near_out, near_stats = rest[-4:]
    up = flags_ref[0] == 1
    seen = {
        (distance, slot): crossing_flags(flags_ref, distance, slot, pair_count)
        for distance in range(2)
        for slot in range(pair_count)
    }
    own_stats[...] = jnp.zeros_like(own_stats)
    near_stats[...] = jnp.zeros_like(near_stats)
    for head in range(head_count):
        columns = head_columns(head)
        keys, values = crossing_keys(own_k, own_v, prior_kv, base, head, head_count)
        for slot in range(pair_count):
            rows = stretch_rows(slot)
            index = slot * head_count + head
            query = pick(up, (backward_q, forward_q), rows, columns)
            near_out[rows, columns], near_stats[index : index + 1, :] = attend(
                query, keys, values, seen[1, slot]
            )
            query = own_q[rows, head_columns(base + head)]
            own_out[rows, columns], own_stats[index : index + 1, :] = attend(
                query, keys, values, seen[0, slot]
            )


def keys_moved_kernel(
    head_count, flags_ref, own_q, own_k, own_v, next_q, *rest, base, pair_count, counts
):
    own_out, own_stats, next_payload = rest[-3:]
    up = flags_ref[0] == 1
    parts = len(counts)
    came = [
        [rest[2 * (hop * parts + part) : 2 * (hop * parts + part) + 2] for part in range(parts)]
        for hop in range(REACH)
    ]

    def moved_block(hop, unit):
        part = 0
        while unit >= counts[part]:
            unit -= counts[part]
            part += 1
        return pick(up, came[hop][part], slice(None), head_columns(unit))

    seen = {
        (ahead, slot): moved_flags(flags_ref, ahead, slot, pair_count)
        for ahead in range(2)
        for slot in range(pair_count)
    }
    own_stats[...] = jnp.zeros_like(own_stats)
    next_stats = [jnp.zeros((1, BLOCK), jnp.float32)] * STAT_ROWS
    for head in range(head_count):
        columns, own_columns = head_columns(head), head_columns(base + head)
        keys = jnp.concatenate(
            [own_k[:, own_columns]] + [moved_block(hop, head) for hop in range(REACH)], axis=0
        )
        values = jnp.transpose(
            jnp.concatenate(
                [own_v[:, own_columns]]
                + [moved_block(hop, head_count + head) for hop in range(REACH)],
                axis=0,
            )
        )
        for slot in range(pair_count):
            rows = stretch_rows(slot)
            index = slot * head_count + head
            attended, next_stats[index] = attend(
                next_q[rows, columns], keys, values, seen[1, slot]
            )
            next_payload[rows, columns] = attended.astype(jnp.bfloat16)
            own_out[rows, columns], own_stats[index : index + 1, :] = attend(
                own_q[rows, own_columns], keys, values, seen[0, slot]
            )
    put_stats(next_payload, jnp.concatenate(next_stats, axis=0), pair_count * BLOCK)


def joined(sender_index, local_out, local_stats, payload_ref, head_count):
    token_rows = local_out.shape[0]
    local_log = local_stats[...]
    remote_log = jnp.where(sender_index > 0, get_stats(payload_ref, token_rows), HIDDEN)
    top = jnp.maximum(local_log, remote_log)
    local_weight = jnp.exp2(local_log - top)
    remote_weight = jnp.exp2(remote_log - top)
    both = local_weight + remote_weight
    scale = 1.0 / both
    local_weight = local_weight * scale
    remote_weight = remote_weight * scale
    parts = {}
    for slot in range(token_rows // BLOCK):
        for head in range(head_count):
            index = slot * head_count + head
            rows, columns = stretch_rows(slot), head_columns(head)
            parts[slot, head] = (
                local_out[rows, columns] * local_weight[index : index + 1]
                + payload_ref[rows, columns].astype(jnp.float32)
                * remote_weight[index : index + 1]
            )
    return parts, top + jnp.log2(both)


def relay_kernel(
    head_count, place_ref, local_out, local_stats, payload_in, *rest, axis
):
    payload_out, stats_out = rest[-2:]
    parts, log_total = joined(place_ref[axis], local_out, local_stats, payload_in, head_count)
    for (slot, head), part in parts.items():
        payload_out[stretch_rows(slot), head_columns(head)] = part.astype(jnp.bfloat16)
    stats_out[...] = log_total
    put_stats(payload_out, log_total, local_out.shape[0])


def finish_kernel(
    head_count, place_ref, local_out, local_stats, payload_in, gates, squares_in, *rest, axis, base
):
    out, squares_out = rest[-2:]
    parts, _ = joined(place_ref[axis], local_out, local_stats, payload_in, head_count)
    squares_out[...] = squares_in[...]
    for slot in range(local_out.shape[0] // BLOCK):
        total = jnp.zeros((1, BLOCK), jnp.float32)
        for head in range(head_count):
            part = parts[slot, head]
            total = total + jnp.sum(part * part, axis=0, keepdims=True)
            gate_row = gates[slot : slot + 1, head_columns(base + head)]
            out[stretch_rows(slot), head_columns(head)] = jnp.transpose(part) * gate_row
        squares_out[slot : slot + 1, :] += total


def scale_kernel(head_counts, feature_count, device_count, *refs):
    squares = sum(ref[...] for ref in refs[:device_count])
    parts, out = refs[device_count:-1], refs[-1]
    factors = as_columns(lax.rsqrt(squares / feature_count + 1e-06))
    for slot in range(out.shape[0] // BLOCK):
        rows = stretch_rows(slot)
        factor = factors[:, slot : slot + 1]
        base = 0
        for part, head_count in zip(parts, head_counts):
            for head in range(head_count):
                out[rows, head_columns(base + head)] = (
                    part[rows, head_columns(head)] * factor
                ).astype(jnp.bfloat16)
            base += head_count


def cost(microseconds):
    return pl.CostEstimate(
        flops=int(microseconds * 1e9), bytes_accessed=int(microseconds * 1e6), transcendentals=0
    )


SMEM = pl.BlockSpec(memory_space=pltpu.SMEM)
VMEM = pl.BlockSpec(memory_space=pltpu.VMEM)
PARAMS = pltpu.CompilerParams(vmem_limit_bytes=32 * 1024 * 1024)


def on_device(query_rows, key_rows, value_rows, gate_table, levels, kv_ranges):
    pair_count, row_count, width_dev = query_rows.shape
    assert row_count == BLOCK
    token_rows = pair_count * row_count
    head_total = width_dev // HEAD_DIM
    place = jnp.stack(
        [
            lax.axis_index("stretch"),
            lax.axis_index("cp"),
            jnp.int32(kv_ranges.shape[1]),
            jnp.int32(kv_ranges.shape[2]),
            goes_up(),
        ]
    ).astype(jnp.int32)
    queries, keys, values = (
        array.reshape(token_rows, width_dev) for array in (query_rows, key_rows, value_rows)
    )
    head_counts = CHUNKS + (KEYS_MOVED,)
    assert sum(head_counts) == head_total and 2 * KEYS_MOVED == sum(CHUNKS)
    assert lax.axis_size("stretch") == 2
    bases = [sum(head_counts[:i]) for i in range(len(head_counts))]
    widths = [count * HEAD_DIM for count in head_counts]
    chunks = range(len(CHUNKS))
    last = len(CHUNKS)

    def float_shape(chunk):
        return jax.ShapeDtypeStruct((token_rows, widths[chunk]), jnp.float32)

    def payload_shape(chunk):
        return jax.ShapeDtypeStruct((token_rows + STAT_ROWS, widths[chunk]), jnp.bfloat16)

    stats_shape = jax.ShapeDtypeStruct((STAT_ROWS, BLOCK), jnp.float32)
    squares_shape = jax.ShapeDtypeStruct((8, BLOCK), jnp.float32)

    def run(name, kernel, chunk, microseconds, out_shape, smem, vmem, after=()):
        return pl.pallas_call(
            functools.partial(kernel, head_counts[chunk]),
            out_shape=out_shape,
            in_specs=[SMEM] * len(smem)
            + [VMEM] * len(vmem)
            + [pl.BlockSpec(memory_space=pl.ANY)] * len(after),
            out_specs=(VMEM,) * len(out_shape),
            compiler_params=PARAMS,
            cost_estimate=cost(microseconds),
            name=name,
        )(*smem, *vmem, *after)

    def block_shape(units):
        return jax.ShapeDtypeStruct((token_rows, units * HEAD_DIM), jnp.bfloat16)

    packed = pl.pallas_call(
        functools.partial(pack_kernel, CHUNKS, KEYS_MOVED),
        out_shape=(block_shape(head_total),) * 3
        + tuple(block_shape(units) for count in CHUNKS for units in (2 * count, count, count)),
        in_specs=[SMEM] + [pl.BlockSpec(memory_space=pltpu.HBM)] * 3,
        out_specs=(VMEM,) * (3 + 3 * len(CHUNKS)),
        scratch_shapes=[pltpu.SemaphoreType.DMA((3,))],
        compiler_params=pltpu.CompilerParams(vmem_limit_bytes=PACK_LIMIT),
        cost_estimate=cost(1.0),
        name="pack",
    )(place, queries, keys, values)
    queries, keys, values = packed[:3]
    prior_kv, hops = [], [[], []]
    for i in chunks:
        crossing, forward, backward = packed[3 * i + 3 : 3 * i + 6]
        prior_kv.append(exchanged(crossing))
        hops[0].append((round_trip(forward, True), round_trip(backward, False)))
    for i in chunks:
        forward, backward = hops[0][i]
        hops[1].append((round_trip(forward, True), round_trip(backward, False)))

    own_parts, near_parts, arrived = [], [], []
    gates, flags = pl.pallas_call(
        functools.partial(plan_kernel, pair_count),
        out_shape=(
            jax.ShapeDtypeStruct((8, width_dev), jnp.float32),
            jax.ShapeDtypeStruct((FLAGS,), jnp.int32),
        ),
        in_specs=[SMEM] * 3 + [VMEM],
        out_specs=(VMEM, SMEM),
        compiler_params=PARAMS,
        cost_estimate=cost(0.6),
        name="plan",
    )(place, kv_ranges, levels, gate_table)
    turn = ()
    for i in chunks:
        near = run(
            "near",
            functools.partial(near_kernel, base=bases[i], pair_count=pair_count),
            i,
            NEAR_COST[i],
            (float_shape(i), stats_shape) * 2,
            (flags,),
            (queries, keys, values, *hops[0][i], prior_kv[i]),
            turn,
        )
        own_parts.append(near[:2])
        near_parts.append(near[2:])
        far_payload, far_stats = run(
            "far",
            functools.partial(far_kernel, base=bases[i], pair_count=pair_count),
            i,
            FAR_COST[i],
            (payload_shape(i), stats_shape),
            (flags,),
            (keys, values, *hops[1][i], prior_kv[i]),
            (near[1],),
        )
        turn = (far_stats,)
        arrived.append(passed_up(far_payload, True))
    own_out, own_stats, next_payload = run(
        "keys_moved",
        functools.partial(
            keys_moved_kernel, base=bases[last], pair_count=pair_count, counts=CHUNKS
        ),
        last,
        KEYS_COST,
        (float_shape(last), stats_shape, payload_shape(last)),
        (flags,),
        (queries, keys, values, prior_kv[0], *[ref for hop in hops for pair in hop for ref in pair]),
        turn,
    )
    own_parts.append((own_out, own_stats))
    turn = (own_stats,)
    arrived.append(exchanged(next_payload))
    for i in chunks:
        relayed, relayed_stats = run(
            "relay",
            functools.partial(relay_kernel, axis=1),
            i,
            0.7,
            (payload_shape(i), stats_shape),
            (place,),
            (*near_parts[i], arrived[i]),
            turn,
        )
        turn = (relayed_stats,)
        arrived[i] = passed_up(relayed, i == 0)
    squares = jnp.zeros(squares_shape.shape, jnp.float32)
    finished = [None] * len(head_counts)
    for i in FINISH_ORDER:
        finished[i], squares = run(
            "finish",
            functools.partial(finish_kernel, axis=0 if i == last else 1, base=bases[i]),
            i,
            0.8,
            (float_shape(i), squares_shape),
            (place,),
            (*own_parts[i], arrived[i], gates, squares),
            turn,
        )
    device_count = lax.axis_size("tp")
    shares = [squares]
    for distance in range(1, device_count):
        route = [(i, (i + distance) % device_count) for i in range(device_count)]
        shares.append(lax.ppermute(squares, "tp", route))
    out = pl.pallas_call(
        functools.partial(scale_kernel, head_counts, float(HEADS * HEAD_DIM), device_count),
        out_shape=jax.ShapeDtypeStruct((token_rows, width_dev), jnp.bfloat16),
        in_specs=[VMEM] * (device_count + len(finished)),
        out_specs=VMEM,
        compiler_params=PARAMS,
        name="scale",
    )(*shares, *finished)
    return out.reshape(query_rows.shape)


def solution(mesh):
    in_specs = (
        P("stretch", "cp", "tp"),
        P("stretch", "cp", "tp"),
        P("stretch", "cp", "tp"),
        P(None, "tp"),
        P(),
        P(),
    )
    out_specs = P("stretch", "cp", "tp")
    return jax.shard_map(
        on_device, mesh=mesh, in_specs=in_specs, out_specs=out_specs, check_vma=False
    )
```

```python
import functools
import math

import jax
import jax.numpy as jnp
from jax import lax
from jax.experimental import pallas as pl
from jax.experimental.pallas import tpu as pltpu
from jax.sharding import PartitionSpec as P

HEADS = 48
HEAD_DIM = 128
BLOCK = 128
REACH = 2
CHUNKS = (5, 3)
KEYS_MOVED = 4
FINISH_ORDER = (2, 0, 1)
WRAP = True
NEAR_COST = (3.0, 1.8)
FAR_COST = (1.5, 0.9)
KEYS_COST = 2.0
PACK_LIMIT = 49 * 1024 * 1024
STAT_ROWS = 16
FLAGS = 64
HIDDEN = -1e30
EXPONENT_SCALE = math.log2(math.e) / math.sqrt(HEAD_DIM)


def exchanged(block):
    return lax.ppermute(block, "stretch", [(0, 1), (1, 0)])


def goes_up():
    return lax.axis_index("tp") < lax.axis_size("tp") // 2


def round_trip(block, forward):
    count, half = lax.axis_size("cp"), lax.axis_size("tp") // 2
    route = []
    for lane in range(half):
        cycle = [i * 2 * half + lane for i in range(count)]
        cycle += [i * 2 * half + half + lane for i in reversed(range(count))]
        route += zip(cycle, cycle[1:] + cycle[:1])
    if not forward:
        route = [(target, source) for source, target in route]
    return lax.ppermute(block, ("cp", "tp"), route)


def passed_up(block, wrap):
    count = lax.axis_size("cp")
    route = [(i, (i + 1) % count) for i in range(count if wrap else count - 1)]
    return lax.ppermute(block, "cp", route)


def head_columns(head):
    return slice(head * HEAD_DIM, (head + 1) * HEAD_DIM)


def stretch_rows(slot):
    return slice(slot * BLOCK, (slot + 1) * BLOCK)


def as_columns(rows):
    fill = jnp.zeros((BLOCK - rows.shape[0], BLOCK), jnp.float32)
    return jnp.transpose(jnp.concatenate([rows, fill], axis=0))


def put_stats(payload_ref, stats, token_rows):
    high = stats.astype(jnp.bfloat16)
    rest = stats - high.astype(jnp.float32)
    middle = rest.astype(jnp.bfloat16)
    low = (rest - middle.astype(jnp.float32)).astype(jnp.bfloat16)
    rows = slice(token_rows, token_rows + STAT_ROWS)
    for index, piece in enumerate((high, middle, low)):
        payload_ref[rows, head_columns(index)] = piece


def get_stats(payload_ref, token_rows):
    rows = slice(token_rows, token_rows + STAT_ROWS)
    pieces = [
        payload_ref[rows, head_columns(index)].astype(jnp.float32) for index in range(3)
    ]
    return (pieces[0] + pieces[1]) + pieces[2]


def shown(place_ref, ranges_ref, query_stretch, query_block, key_stretch, key_block):
    stretch_count, block_count = place_ref[2], place_ref[3]
    low, high = (
        ranges_ref[
            end,
            jnp.minimum(query_stretch, stretch_count - 1),
            jnp.minimum(query_block, block_count - 1),
            jnp.maximum(key_stretch, 0),
        ]
        for end in range(2)
    )
    exists = (
        (query_stretch < stretch_count)
        & (query_block < block_count)
        & (key_stretch >= 0)
        & (key_block >= 0)
    )
    return exists & (low <= key_block) & (key_block < high)


def attend(query, keys, values, seen):
    scores = lax.dot_general(
        keys, query, (((1,), (1,)), ((), ())), preferred_element_type=jnp.float32
    )
    blocks = [scores[stretch_rows(j)] for j in range(len(seen))]
    peak = jnp.full((1, BLOCK), HIDDEN, jnp.float32)
    for block, flag in zip(blocks, seen):
        block_peak = jnp.max(block, axis=0, keepdims=True)
        peak = jnp.maximum(peak, jnp.where(flag, block_peak, HIDDEN))
    shift = peak * EXPONENT_SCALE
    weights = [
        jnp.exp2(block * EXPONENT_SCALE - jnp.where(flag, shift, -HIDDEN))
        for block, flag in zip(blocks, seen)
    ]
    total = sum(jnp.sum(weight, axis=0, keepdims=True) for weight in weights)
    weights = jnp.concatenate([weight.astype(jnp.bfloat16) for weight in weights], axis=0)
    summed = jnp.dot(values, weights, preferred_element_type=jnp.float32)
    total = jnp.maximum(total, 1e-30)
    return summed * (1.0 / total), jnp.maximum(shift + jnp.log2(total), HIDDEN)


def pick(up, refs, *index):
    return jnp.where(up, refs[0][index], refs[1][index])


def pack_kernel(counts, keys_moved, place_ref, q_hbm, k_hbm, v_hbm, *refs):
    base = sum(counts)
    q_ref, k_ref, v_ref = refs[:3]
    outs, semaphores = refs[3:-1], refs[-1]
    copies = [
        pltpu.make_async_copy(source, target, semaphores.at[index])
        for index, (source, target) in enumerate(
            ((q_hbm, q_ref), (k_hbm, k_ref), (v_hbm, v_ref))
        )
    ]
    for copy in copies:
        copy.start()
    columns = [head_columns(head) for head in range(base + keys_moved)]
    moving = [(ref, part) for ref in (k_ref, v_ref) for part in columns[base:]]
    up = place_ref[4] == 1
    last_group = place_ref[0] > 0
    bounds = [sum(counts[:i]) for i in range(len(counts) + 1)]

    def fill(out, parts, source):
        for index, (ref, part) in enumerate(parts):
            if ref is source:
                out[:, head_columns(index)] = ref[:, part]

    for copy, source in zip(copies, (q_ref, k_ref, v_ref)):
        copy.wait()
        jobs = []
        for i, (start, stop) in enumerate(zip(bounds, bounds[1:])):
            own = columns[start:stop]
            jobs.append(
                (
                    *outs[3 * i : 3 * i + 3],
                    [(ref, part) for ref in (k_ref, v_ref) for part in own],
                    [(q_ref, part) for part in own],
                    moving[start:stop],
                )
            )

        @pl.when(up)
        def _():
            for _, forward_out, backward_out, _, queries, keys in jobs:
                fill(forward_out, keys, source)
                fill(backward_out, queries, source)

        @pl.when(jnp.logical_not(up))
        def _():
            for _, forward_out, backward_out, _, queries, keys in jobs:
                fill(forward_out, queries, source)
                fill(backward_out, keys, source)

        for cross_out, _, _, crossing, _, _ in jobs:
            fill(cross_out, crossing, source)

    @pl.when(last_group)
    def _():
        fill(outs[0], [(q_ref, part) for part in columns[base:]], q_ref)


def crossing_keys(own_k, own_v, prior_kv, base, head, head_count):
    own_columns = head_columns(base + head)
    keys = jnp.concatenate([own_k[:, own_columns], prior_kv[:, head_columns(head)]], axis=0)
    values = jnp.concatenate(
        [own_v[:, own_columns], prior_kv[:, head_columns(head_count + head)]], axis=0
    )
    return keys, jnp.transpose(values)


def plan_kernel(pair_count, place_ref, ranges_ref, levels_ref, gate_table, *rest):
    gates_out, flags_out = rest[-2:]
    gates = gate_table[...].astype(jnp.float32)
    level_ids = lax.broadcasted_iota(jnp.int32, gates.shape, 0)
    gates_out[...] = jnp.zeros_like(gates_out)
    for slot in range(pair_count):
        level = levels_ref[place_ref[0] * pair_count + slot]
        gates_out[slot : slot + 1, :] = jnp.sum(
            jnp.where(level_ids == level, gates, 0.0), axis=0, keepdims=True
        )
    group, position = place_ref[0], place_ref[1]
    flags_out[0] = place_ref[4]
    index = 1
    for distance in range(REACH + 1):
        for slot in range(pair_count):
            for behind in range(2):
                for key_slot in range(pair_count):
                    flag = shown(
                        place_ref,
                        ranges_ref,
                        group * pair_count + slot,
                        position + distance,
                        (group - behind) * pair_count + key_slot,
                        position,
                    )
                    flags_out[index] = flag.astype(jnp.int32)
                    index += 1
    for ahead in range(2):
        for slot in range(pair_count):
            for distance in range(REACH + 1):
                for key_slot in range(pair_count):
                    flag = shown(
                        place_ref,
                        ranges_ref,
                        (group + ahead) * pair_count + slot,
                        position,
                        group * pair_count + key_slot,
                        position - distance,
                    )
                    flags_out[index] = flag.astype(jnp.int32)
                    index += 1


def crossing_flags(flags_ref, distance, slot, pair_count):
    base = 1 + (distance * pair_count + slot) * 2 * pair_count
    return [flags_ref[base + j] == 1 for j in range(2 * pair_count)]


def moved_flags(flags_ref, ahead, slot, pair_count):
    count = (REACH + 1) * pair_count
    base = 1 + count * 2 * pair_count + (ahead * pair_count + slot) * count
    return [flags_ref[base + j] == 1 for j in range(count)]


def far_kernel(
    head_count, flags_ref, own_k, own_v, forward_q, backward_q, prior_kv, *rest,
    base, pair_count,
):
    far_payload, far_stats = rest[-2:]
    up = flags_ref[0] == 1
    seen = [crossing_flags(flags_ref, 2, slot, pair_count) for slot in range(pair_count)]
    stats = [jnp.zeros((1, BLOCK), jnp.float32)] * STAT_ROWS
    for head in range(head_count):
        columns = head_columns(head)
        keys, values = crossing_keys(own_k, own_v, prior_kv, base, head, head_count)
        for slot in range(pair_count):
            rows = stretch_rows(slot)
            query = pick(up, (backward_q, forward_q), rows, columns)
            attended, stats[slot * head_count + head] = attend(query, keys, values, seen[slot])
            far_payload[rows, columns] = attended.astype(jnp.bfloat16)
    far_stats[...] = jnp.concatenate(stats, axis=0)
    put_stats(far_payload, far_stats[...], pair_count * BLOCK)


def near_kernel(
    head_count, flags_ref, own_q, own_k, own_v, forward_q, backward_q, prior_kv,
    *rest, base, pair_count,
):
    own_out, own_stats, near_out, near_stats = rest[-4:]
    up = flags_ref[0] == 1
    seen = {
        (distance, slot): crossing_flags(flags_ref, distance, slot, pair_count)
        for distance in range(2)
        for slot in range(pair_count)
    }
    own_stats[...] = jnp.zeros_like(own_stats)
    near_stats[...] = jnp.zeros_like(near_stats)
    for head in range(head_count):
        columns = head_columns(head)
        keys, values = crossing_keys(own_k, own_v, prior_kv, base, head, head_count)
        for slot in range(pair_count):
            rows = stretch_rows(slot)
            index = slot * head_count + head
            query = pick(up, (backward_q, forward_q), rows, columns)
            near_out[rows, columns], near_stats[index : index + 1, :] = attend(
                query, keys, values, seen[1, slot]
            )
            query = own_q[rows, head_columns(base + head)]
            own_out[rows, columns], own_stats[index : index + 1, :] = attend(
                query, keys, values, seen[0, slot]
            )


def keys_moved_kernel(
    head_count, flags_ref, own_q, own_k, own_v, next_q, *rest, base, pair_count, counts
):
    own_out, own_stats, next_payload = rest[-3:]
    up = flags_ref[0] == 1
    parts = len(counts)
    came = [
        [rest[2 * (hop * parts + part) : 2 * (hop * parts + part) + 2] for part in range(parts)]
        for hop in range(REACH)
    ]

    def moved_block(hop, unit):
        part = 0
        while unit >= counts[part]:
            unit -= counts[part]
            part += 1
        return pick(up, came[hop][part], slice(None), head_columns(unit))

    seen = {
        (ahead, slot): moved_flags(flags_ref, ahead, slot, pair_count)
        for ahead in range(2)
        for slot in range(pair_count)
    }
    own_stats[...] = jnp.zeros_like(own_stats)
    next_stats = [jnp.zeros((1, BLOCK), jnp.float32)] * STAT_ROWS
    for head in range(head_count):
        columns, own_columns = head_columns(head), head_columns(base + head)
        keys = jnp.concatenate(
            [own_k[:, own_columns]] + [moved_block(hop, head) for hop in range(REACH)], axis=0
        )
        values = jnp.transpose(
            jnp.concatenate(
                [own_v[:, own_columns]]
                + [moved_block(hop, head_count + head) for hop in range(REACH)],
                axis=0,
            )
        )
        for slot in range(pair_count):
            rows = stretch_rows(slot)
            index = slot * head_count + head
            attended, next_stats[index] = attend(
                next_q[rows, columns], keys, values, seen[1, slot]
            )
            next_payload[rows, columns] = attended.astype(jnp.bfloat16)
            own_out[rows, columns], own_stats[index : index + 1, :] = attend(
                own_q[rows, own_columns], keys, values, seen[0, slot]
            )
    put_stats(next_payload, jnp.concatenate(next_stats, axis=0), pair_count * BLOCK)


def joined(sender_index, local_out, local_stats, payload_ref, head_count):
    token_rows = local_out.shape[0]
    local_log = local_stats[...]
    remote_log = jnp.where(sender_index > 0, get_stats(payload_ref, token_rows), HIDDEN)
    top = jnp.maximum(local_log, remote_log)
    local_weight = jnp.exp2(local_log - top)
    remote_weight = jnp.exp2(remote_log - top)
    both = local_weight + remote_weight
    scale = 1.0 / both
    local_weight = local_weight * scale
    remote_weight = remote_weight * scale
    parts = {}
    for slot in range(token_rows // BLOCK):
        for head in range(head_count):
            index = slot * head_count + head
            rows, columns = stretch_rows(slot), head_columns(head)
            parts[slot, head] = (
                local_out[rows, columns] * local_weight[index : index + 1]
                + payload_ref[rows, columns].astype(jnp.float32)
                * remote_weight[index : index + 1]
            )
    return parts, top + jnp.log2(both)


def relay_kernel(
    head_count, place_ref, local_out, local_stats, payload_in, *rest, axis
):
    payload_out, stats_out = rest[-2:]
    parts, log_total = joined(place_ref[axis], local_out, local_stats, payload_in, head_count)
    for (slot, head), part in parts.items():
        payload_out[stretch_rows(slot), head_columns(head)] = part.astype(jnp.bfloat16)
    stats_out[...] = log_total
    put_stats(payload_out, log_total, local_out.shape[0])


def finish_kernel(
    head_count, place_ref, local_out, local_stats, payload_in, gates, squares_in, *rest, axis, base
):
    out, squares_out = rest[-2:]
    parts, _ = joined(place_ref[axis], local_out, local_stats, payload_in, head_count)
    squares_out[...] = squares_in[...]
    for slot in range(local_out.shape[0] // BLOCK):
        total = jnp.zeros((1, BLOCK), jnp.float32)
        for head in range(head_count):
            part = parts[slot, head]
            total = total + jnp.sum(part * part, axis=0, keepdims=True)
            gate_row = gates[slot : slot + 1, head_columns(base + head)]
            out[stretch_rows(slot), head_columns(head)] = jnp.transpose(part) * gate_row
        squares_out[slot : slot + 1, :] += total


def scale_kernel(head_counts, feature_count, device_count, *refs):
    squares = sum(ref[...] for ref in refs[:device_count])
    parts, out = refs[device_count:-1], refs[-1]
    factors = as_columns(lax.rsqrt(squares / feature_count + 1e-06))
    for slot in range(out.shape[0] // BLOCK):
        rows = stretch_rows(slot)
        factor = factors[:, slot : slot + 1]
        base = 0
        for part, head_count in zip(parts, head_counts):
            for head in range(head_count):
                out[rows, head_columns(base + head)] = (
                    part[rows, head_columns(head)] * factor
                ).astype(jnp.bfloat16)
            base += head_count


def cost(microseconds):
    return pl.CostEstimate(
        flops=int(microseconds * 1e9), bytes_accessed=int(microseconds * 1e6), transcendentals=0
    )


SMEM = pl.BlockSpec(memory_space=pltpu.SMEM)
VMEM = pl.BlockSpec(memory_space=pltpu.VMEM)
PARAMS = pltpu.CompilerParams(vmem_limit_bytes=32 * 1024 * 1024)


def on_device(query_rows, key_rows, value_rows, gate_table, levels, kv_ranges):
    pair_count, row_count, width_dev = query_rows.shape
    assert row_count == BLOCK
    token_rows = pair_count * row_count
    head_total = width_dev // HEAD_DIM
    place = jnp.stack(
        [
            lax.axis_index("stretch"),
            lax.axis_index("cp"),
            jnp.int32(kv_ranges.shape[1]),
            jnp.int32(kv_ranges.shape[2]),
            goes_up(),
        ]
    ).astype(jnp.int32)
    queries, keys, values = (
        array.reshape(token_rows, width_dev) for array in (query_rows, key_rows, value_rows)
    )
    head_counts = CHUNKS + (KEYS_MOVED,)
    assert sum(head_counts) == head_total and 2 * KEYS_MOVED == sum(CHUNKS)
    assert lax.axis_size("stretch") == 2
    bases = [sum(head_counts[:i]) for i in range(len(head_counts))]
    widths = [count * HEAD_DIM for count in head_counts]
    chunks = range(len(CHUNKS))
    last = len(CHUNKS)

    def float_shape(chunk):
        return jax.ShapeDtypeStruct((token_rows, widths[chunk]), jnp.float32)

    def payload_shape(chunk):
        return jax.ShapeDtypeStruct((token_rows + STAT_ROWS, widths[chunk]), jnp.bfloat16)

    stats_shape = jax.ShapeDtypeStruct((STAT_ROWS, BLOCK), jnp.float32)
    squares_shape = jax.ShapeDtypeStruct((8, BLOCK), jnp.float32)

    def run(name, kernel, chunk, microseconds, out_shape, smem, vmem, after=()):
        return pl.pallas_call(
            functools.partial(kernel, head_counts[chunk]),
            out_shape=out_shape,
            in_specs=[SMEM] * len(smem)
            + [VMEM] * len(vmem)
            + [pl.BlockSpec(memory_space=pl.ANY)] * len(after),
            out_specs=(VMEM,) * len(out_shape),
            compiler_params=PARAMS,
            cost_estimate=cost(microseconds),
            name=name,
        )(*smem, *vmem, *after)

    def block_shape(units):
        return jax.ShapeDtypeStruct((token_rows, units * HEAD_DIM), jnp.bfloat16)

    packed = pl.pallas_call(
        functools.partial(pack_kernel, CHUNKS, KEYS_MOVED),
        out_shape=(block_shape(head_total),) * 3
        + tuple(block_shape(units) for count in CHUNKS for units in (2 * count, count, count)),
        in_specs=[SMEM] + [pl.BlockSpec(memory_space=pltpu.HBM)] * 3,
        out_specs=(VMEM,) * (3 + 3 * len(CHUNKS)),
        scratch_shapes=[pltpu.SemaphoreType.DMA((3,))],
        compiler_params=pltpu.CompilerParams(vmem_limit_bytes=PACK_LIMIT),
        cost_estimate=cost(1.0),
        name="pack",
    )(place, queries, keys, values)
    queries, keys, values = packed[:3]
    prior_kv, hops = [], [[], []]
    for i in chunks:
        crossing, forward, backward = packed[3 * i + 3 : 3 * i + 6]
        prior_kv.append(exchanged(crossing))
        hops[0].append((round_trip(forward, True), round_trip(backward, False)))
    for i in chunks:
        forward, backward = hops[0][i]
        hops[1].append((round_trip(forward, True), round_trip(backward, False)))

    own_parts, near_parts, arrived = [], [], []
    gates, flags = pl.pallas_call(
        functools.partial(plan_kernel, pair_count),
        out_shape=(
            jax.ShapeDtypeStruct((8, width_dev), jnp.float32),
            jax.ShapeDtypeStruct((FLAGS,), jnp.int32),
        ),
        in_specs=[SMEM] * 3 + [VMEM],
        out_specs=(VMEM, SMEM),
        compiler_params=PARAMS,
        cost_estimate=cost(0.6),
        name="plan",
    )(place, kv_ranges, levels, gate_table)
    turn = ()
    for i in chunks:
        near = run(
            "near",
            functools.partial(near_kernel, base=bases[i], pair_count=pair_count),
            i,
            NEAR_COST[i],
            (float_shape(i), stats_shape) * 2,
            (flags,),
            (queries, keys, values, *hops[0][i], prior_kv[i]),
            turn,
        )
        own_parts.append(near[:2])
        near_parts.append(near[2:])
        far_payload, far_stats = run(
            "far",
            functools.partial(far_kernel, base=bases[i], pair_count=pair_count),
            i,
            FAR_COST[i],
            (payload_shape(i), stats_shape),
            (flags,),
            (keys, values, *hops[1][i], prior_kv[i]),
            (near[1],),
        )
        turn = (far_stats,)
        arrived.append(passed_up(far_payload, True))
    own_out, own_stats, next_payload = run(
        "keys_moved",
        functools.partial(
            keys_moved_kernel, base=bases[last], pair_count=pair_count, counts=CHUNKS
        ),
        last,
        KEYS_COST,
        (float_shape(last), stats_shape, payload_shape(last)),
        (flags,),
        (queries, keys, values, prior_kv[0], *[ref for hop in hops for pair in hop for ref in pair]),
        turn,
    )
    own_parts.append((own_out, own_stats))
    turn = (own_stats,)
    arrived.append(exchanged(next_payload))
    for i in chunks:
        relayed, relayed_stats = run(
            "relay",
            functools.partial(relay_kernel, axis=1),
            i,
            0.7,
            (payload_shape(i), stats_shape),
            (place,),
            (*near_parts[i], arrived[i]),
            turn,
        )
        turn = (relayed_stats,)
        arrived[i] = passed_up(relayed, i == 0)
    squares = jnp.zeros(squares_shape.shape, jnp.float32)
    finished = [None] * len(head_counts)
    for i in FINISH_ORDER:
        finished[i], squares = run(
            "finish",
            functools.partial(finish_kernel, axis=0 if i == last else 1, base=bases[i]),
            i,
            0.8,
            (float_shape(i), squares_shape),
            (place,),
            (*own_parts[i], arrived[i], gates, squares),
            turn,
        )
    device_count = lax.axis_size("tp")
    assert device_count & (device_count - 1) == 0
    shares = [squares]
    for distance in range(1, device_count):
        route = [(i, i ^ distance) for i in range(device_count)]
        shares.append(lax.ppermute(squares, "tp", route))
    out = pl.pallas_call(
        functools.partial(scale_kernel, head_counts, float(HEADS * HEAD_DIM), device_count),
        out_shape=jax.ShapeDtypeStruct((token_rows, width_dev), jnp.bfloat16),
        in_specs=[VMEM] * (device_count + len(finished)),
        out_specs=VMEM,
        compiler_params=PARAMS,
        name="scale",
    )(*shares, *finished)
    return out.reshape(query_rows.shape)


def solution(mesh):
    in_specs = (
        P("stretch", "cp", "tp"),
        P("stretch", "cp", "tp"),
        P("stretch", "cp", "tp"),
        P(None, "tp"),
        P(),
        P(),
    )
    out_specs = P("stretch", "cp", "tp")
    return jax.shard_map(
        on_device, mesh=mesh, in_specs=in_specs, out_specs=out_specs, check_vma=False
    )
```

```python
import functools
import math

import jax
import jax.numpy as jnp
from jax import lax
from jax.experimental import pallas as pl
from jax.experimental.pallas import tpu as pltpu
from jax.sharding import PartitionSpec as P

HEADS = 48
HEAD_DIM = 128
BLOCK = 128
REACH = 2
CHUNKS = (5, 3)
KEYS_MOVED = 4
FINISH_ORDER = (2, 0, 1)
WRAP = True
NEAR_COST = (3.0, 1.8)
FAR_COST = (1.5, 0.9)
KEYS_COST = 2.0
PACK_LIMIT = 49 * 1024 * 1024
STAT_ROWS = 16
FLAGS = 64
HIDDEN = -1e30
EXPONENT_SCALE = math.log2(math.e) / math.sqrt(HEAD_DIM)


def exchanged(block):
    return lax.ppermute(block, "stretch", [(0, 1), (1, 0)])


def goes_up():
    return lax.axis_index("tp") < lax.axis_size("tp") // 2


def round_trip(block, forward):
    count, half = lax.axis_size("cp"), lax.axis_size("tp") // 2
    route = []
    for lane in range(half):
        cycle = [i * 2 * half + lane for i in range(count)]
        cycle += [i * 2 * half + half + lane for i in reversed(range(count))]
        route += zip(cycle, cycle[1:] + cycle[:1])
    if not forward:
        route = [(target, source) for source, target in route]
    return lax.ppermute(block, ("cp", "tp"), route)


def passed_up(block, wrap):
    count = lax.axis_size("cp")
    route = [(i, (i + 1) % count) for i in range(count if wrap else count - 1)]
    return lax.ppermute(block, "cp", route)


def head_columns(head):
    return slice(head * HEAD_DIM, (head + 1) * HEAD_DIM)


def stretch_rows(slot):
    return slice(slot * BLOCK, (slot + 1) * BLOCK)


def as_columns(rows):
    fill = jnp.zeros((BLOCK - rows.shape[0], BLOCK), jnp.float32)
    return jnp.transpose(jnp.concatenate([rows, fill], axis=0))


def put_stats(payload_ref, stats, token_rows):
    high = stats.astype(jnp.bfloat16)
    rest = stats - high.astype(jnp.float32)
    middle = rest.astype(jnp.bfloat16)
    low = (rest - middle.astype(jnp.float32)).astype(jnp.bfloat16)
    rows = slice(token_rows, token_rows + STAT_ROWS)
    for index, piece in enumerate((high, middle, low)):
        payload_ref[rows, head_columns(index)] = piece


def get_stats(payload_ref, token_rows):
    rows = slice(token_rows, token_rows + STAT_ROWS)
    pieces = [
        payload_ref[rows, head_columns(index)].astype(jnp.float32) for index in range(3)
    ]
    return (pieces[0] + pieces[1]) + pieces[2]


def shown(place_ref, ranges_ref, query_stretch, query_block, key_stretch, key_block):
    stretch_count, block_count = place_ref[2], place_ref[3]
    low, high = (
        ranges_ref[
            end,
            jnp.minimum(query_stretch, stretch_count - 1),
            jnp.minimum(query_block, block_count - 1),
            jnp.maximum(key_stretch, 0),
        ]
        for end in range(2)
    )
    exists = (
        (query_stretch < stretch_count)
        & (query_block < block_count)
        & (key_stretch >= 0)
        & (key_block >= 0)
    )
    return exists & (low <= key_block) & (key_block < high)


def attend(query, keys, values, seen):
    scores = lax.dot_general(
        keys, query, (((1,), (1,)), ((), ())), preferred_element_type=jnp.float32
    )
    blocks = [scores[stretch_rows(j)] for j in range(len(seen))]
    peak = jnp.full((1, BLOCK), HIDDEN, jnp.float32)
    for block, flag in zip(blocks, seen):
        block_peak = jnp.max(block, axis=0, keepdims=True)
        peak = jnp.maximum(peak, jnp.where(flag, block_peak, HIDDEN))
    shift = peak * EXPONENT_SCALE
    weights = [
        jnp.exp2(block * EXPONENT_SCALE - jnp.where(flag, shift, -HIDDEN))
        for block, flag in zip(blocks, seen)
    ]
    total = sum(jnp.sum(weight, axis=0, keepdims=True) for weight in weights)
    weights = jnp.concatenate([weight.astype(jnp.bfloat16) for weight in weights], axis=0)
    summed = jnp.dot(values, weights, preferred_element_type=jnp.float32)
    total = jnp.maximum(total, 1e-30)
    return summed * (1.0 / total), jnp.maximum(shift + jnp.log2(total), HIDDEN)


def pick(up, refs, *index):
    return jnp.where(up, refs[0][index], refs[1][index])


def pack_kernel(counts, keys_moved, place_ref, q_hbm, k_hbm, v_hbm, *refs):
    base = sum(counts)
    q_ref, k_ref, v_ref = refs[:3]
    outs, semaphores = refs[3:-1], refs[-1]
    copies = [
        pltpu.make_async_copy(source, target, semaphores.at[index])
        for index, (source, target) in enumerate(
            ((q_hbm, q_ref), (k_hbm, k_ref), (v_hbm, v_ref))
        )
    ]
    for copy in copies:
        copy.start()
    columns = [head_columns(head) for head in range(base + keys_moved)]
    moving = [(ref, part) for ref in (k_ref, v_ref) for part in columns[base:]]
    up = place_ref[4] == 1
    last_group = place_ref[0] > 0
    bounds = [sum(counts[:i]) for i in range(len(counts) + 1)]

    def fill(out, parts, source):
        for index, (ref, part) in enumerate(parts):
            if ref is source:
                out[:, head_columns(index)] = ref[:, part]

    for copy, source in zip(copies, (q_ref, k_ref, v_ref)):
        copy.wait()
        jobs = []
        for i, (start, stop) in enumerate(zip(bounds, bounds[1:])):
            own = columns[start:stop]
            jobs.append(
                (
                    *outs[3 * i : 3 * i + 3],
                    [(ref, part) for ref in (k_ref, v_ref) for part in own],
                    [(q_ref, part) for part in own],
                    moving[start:stop],
                )
            )

        @pl.when(up)
        def _():
            for _, forward_out, backward_out, _, queries, keys in jobs:
                fill(forward_out, keys, source)
                fill(backward_out, queries, source)

        @pl.when(jnp.logical_not(up))
        def _():
            for _, forward_out, backward_out, _, queries, keys in jobs:
                fill(forward_out, queries, source)
                fill(backward_out, keys, source)

        for cross_out, _, _, crossing, _, _ in jobs:
            fill(cross_out, crossing, source)

    @pl.when(last_group)
    def _():
        fill(outs[0], [(q_ref, part) for part in columns[base:]], q_ref)


def crossing_keys(own_k, own_v, prior_kv, base, head, head_count):
    own_columns = head_columns(base + head)
    keys = jnp.concatenate([own_k[:, own_columns], prior_kv[:, head_columns(head)]], axis=0)
    values = jnp.concatenate(
        [own_v[:, own_columns], prior_kv[:, head_columns(head_count + head)]], axis=0
    )
    return keys, jnp.transpose(values)


def plan_kernel(pair_count, place_ref, ranges_ref, levels_ref, gate_table, *rest):
    gates_out, flags_out = rest[-2:]
    gates = gate_table[...].astype(jnp.float32)
    level_ids = lax.broadcasted_iota(jnp.int32, gates.shape, 0)
    gates_out[...] = jnp.zeros_like(gates_out)
    for slot in range(pair_count):
        level = levels_ref[place_ref[0] * pair_count + slot]
        gates_out[slot : slot + 1, :] = jnp.sum(
            jnp.where(level_ids == level, gates, 0.0), axis=0, keepdims=True
        )
    group, position = place_ref[0], place_ref[1]
    flags_out[0] = place_ref[4]
    index = 1
    for distance in range(REACH + 1):
        for slot in range(pair_count):
            for behind in range(2):
                for key_slot in range(pair_count):
                    flag = shown(
                        place_ref,
                        ranges_ref,
                        group * pair_count + slot,
                        position + distance,
                        (group - behind) * pair_count + key_slot,
                        position,
                    )
                    flags_out[index] = flag.astype(jnp.int32)
                    index += 1
    for ahead in range(2):
        for slot in range(pair_count):
            for distance in range(REACH + 1):
                for key_slot in range(pair_count):
                    flag = shown(
                        place_ref,
                        ranges_ref,
                        (group + ahead) * pair_count + slot,
                        position,
                        group * pair_count + key_slot,
                        position - distance,
                    )
                    flags_out[index] = flag.astype(jnp.int32)
                    index += 1


def crossing_flags(flags_ref, distance, slot, pair_count):
    base = 1 + (distance * pair_count + slot) * 2 * pair_count
    return [flags_ref[base + j] == 1 for j in range(2 * pair_count)]


def moved_flags(flags_ref, ahead, slot, pair_count):
    count = (REACH + 1) * pair_count
    base = 1 + count * 2 * pair_count + (ahead * pair_count + slot) * count
    return [flags_ref[base + j] == 1 for j in range(count)]


def far_kernel(
    head_count, flags_ref, own_k, own_v, forward_q, backward_q, prior_kv, *rest,
    base, pair_count,
):
    far_payload, far_stats = rest[-2:]
    up = flags_ref[0] == 1
    seen = [crossing_flags(flags_ref, 2, slot, pair_count) for slot in range(pair_count)]
    stats = [jnp.zeros((1, BLOCK), jnp.float32)] * STAT_ROWS
    for head in range(head_count):
        columns = head_columns(head)
        keys, values = crossing_keys(own_k, own_v, prior_kv, base, head, head_count)
        for slot in range(pair_count):
            rows = stretch_rows(slot)
            query = pick(up, (backward_q, forward_q), rows, columns)
            attended, stats[slot * head_count + head] = attend(query, keys, values, seen[slot])
            far_payload[rows, columns] = attended.astype(jnp.bfloat16)
    far_stats[...] = jnp.concatenate(stats, axis=0)
    put_stats(far_payload, far_stats[...], pair_count * BLOCK)


def near_kernel(
    head_count, flags_ref, own_q, own_k, own_v, forward_q, backward_q, prior_kv,
    *rest, base, pair_count,
):
    own_out, own_stats, near_out, near_stats = rest[-4:]
    up = flags_ref[0] == 1
    seen = {
        (distance, slot): crossing_flags(flags_ref, distance, slot, pair_count)
        for distance in range(2)
        for slot in range(pair_count)
    }
    own_stats[...] = jnp.zeros_like(own_stats)
    near_stats[...] = jnp.zeros_like(near_stats)
    for head in range(head_count):
        columns = head_columns(head)
        keys, values = crossing_keys(own_k, own_v, prior_kv, base, head, head_count)
        for slot in range(pair_count):
            rows = stretch_rows(slot)
            index = slot * head_count + head
            query = pick(up, (backward_q, forward_q), rows, columns)
            near_out[rows, columns], near_stats[index : index + 1, :] = attend(
                query, keys, values, seen[1, slot]
            )
            query = own_q[rows, head_columns(base + head)]
            own_out[rows, columns], own_stats[index : index + 1, :] = attend(
                query, keys, values, seen[0, slot]
            )


def keys_moved_kernel(
    head_count, flags_ref, own_q, own_k, own_v, next_q, *rest, base, pair_count, counts
):
    own_out, own_stats, next_payload = rest[-3:]
    up = flags_ref[0] == 1
    parts = len(counts)
    came = [
        [rest[2 * (hop * parts + part) : 2 * (hop * parts + part) + 2] for part in range(parts)]
        for hop in range(REACH)
    ]

    def moved_block(hop, unit):
        part = 0
        while unit >= counts[part]:
            unit -= counts[part]
            part += 1
        return pick(up, came[hop][part], slice(None), head_columns(unit))

    seen = {
        (ahead, slot): moved_flags(flags_ref, ahead, slot, pair_count)
        for ahead in range(2)
        for slot in range(pair_count)
    }
    own_stats[...] = jnp.zeros_like(own_stats)
    next_stats = [jnp.zeros((1, BLOCK), jnp.float32)] * STAT_ROWS
    for head in range(head_count):
        columns, own_columns = head_columns(head), head_columns(base + head)
        keys = jnp.concatenate(
            [own_k[:, own_columns]] + [moved_block(hop, head) for hop in range(REACH)], axis=0
        )
        values = jnp.transpose(
            jnp.concatenate(
                [own_v[:, own_columns]]
                + [moved_block(hop, head_count + head) for hop in range(REACH)],
                axis=0,
            )
        )
        for slot in range(pair_count):
            rows = stretch_rows(slot)
            index = slot * head_count + head
            attended, next_stats[index] = attend(
                next_q[rows, columns], keys, values, seen[1, slot]
            )
            next_payload[rows, columns] = attended.astype(jnp.bfloat16)
            own_out[rows, columns], own_stats[index : index + 1, :] = attend(
                own_q[rows, own_columns], keys, values, seen[0, slot]
            )
    put_stats(next_payload, jnp.concatenate(next_stats, axis=0), pair_count * BLOCK)


def joined(sender_index, local_out, local_stats, payload_ref, head_count):
    token_rows = local_out.shape[0]
    local_log = local_stats[...]
    remote_log = jnp.where(sender_index > 0, get_stats(payload_ref, token_rows), HIDDEN)
    top = jnp.maximum(local_log, remote_log)
    local_weight = jnp.exp2(local_log - top)
    remote_weight = jnp.exp2(remote_log - top)
    both = local_weight + remote_weight
    scale = 1.0 / both
    local_weight = local_weight * scale
    remote_weight = remote_weight * scale
    parts = {}
    for slot in range(token_rows // BLOCK):
        for head in range(head_count):
            index = slot * head_count + head
            rows, columns = stretch_rows(slot), head_columns(head)
            parts[slot, head] = (
                local_out[rows, columns] * local_weight[index : index + 1]
                + payload_ref[rows, columns].astype(jnp.float32)
                * remote_weight[index : index + 1]
            )
    return parts, top + jnp.log2(both)


def relay_kernel(
    head_count, place_ref, local_out, local_stats, payload_in, *rest, axis
):
    payload_out, stats_out = rest[-2:]
    parts, log_total = joined(place_ref[axis], local_out, local_stats, payload_in, head_count)
    for (slot, head), part in parts.items():
        payload_out[stretch_rows(slot), head_columns(head)] = part.astype(jnp.bfloat16)
    stats_out[...] = log_total
    put_stats(payload_out, log_total, local_out.shape[0])


def finish_kernel(
    head_count, place_ref, local_out, local_stats, payload_in, gates, squares_in, *rest, axis, base
):
    out, squares_out = rest[-2:]
    parts, _ = joined(place_ref[axis], local_out, local_stats, payload_in, head_count)
    squares_out[...] = squares_in[...]
    for slot in range(local_out.shape[0] // BLOCK):
        total = jnp.zeros((1, BLOCK), jnp.float32)
        for head in range(head_count):
            part = parts[slot, head]
            total = total + jnp.sum(part * part, axis=0, keepdims=True)
            gate_row = gates[slot : slot + 1, head_columns(base + head)]
            out[stretch_rows(slot), head_columns(head)] = jnp.transpose(part) * gate_row
        squares_out[slot : slot + 1, :] += total


def scale_kernel(head_counts, feature_count, device_count, *refs):
    squares = sum(ref[...] for ref in refs[:device_count])
    parts, out = refs[device_count:-1], refs[-1]
    factors = as_columns(lax.rsqrt(squares / feature_count + 1e-06))
    for slot in range(out.shape[0] // BLOCK):
        rows = stretch_rows(slot)
        factor = factors[:, slot : slot + 1]
        base = 0
        for part, head_count in zip(parts, head_counts):
            for head in range(head_count):
                out[rows, head_columns(base + head)] = (
                    part[rows, head_columns(head)] * factor
                ).astype(jnp.bfloat16)
            base += head_count


def cost(microseconds):
    return pl.CostEstimate(
        flops=int(microseconds * 1e9), bytes_accessed=int(microseconds * 1e6), transcendentals=0
    )


SMEM = pl.BlockSpec(memory_space=pltpu.SMEM)
VMEM = pl.BlockSpec(memory_space=pltpu.VMEM)
PARAMS = pltpu.CompilerParams(vmem_limit_bytes=32 * 1024 * 1024)


def on_device(query_rows, key_rows, value_rows, gate_table, levels, kv_ranges):
    pair_count, row_count, width_dev = query_rows.shape
    assert row_count == BLOCK
    token_rows = pair_count * row_count
    head_total = width_dev // HEAD_DIM
    place = jnp.stack(
        [
            lax.axis_index("stretch"),
            lax.axis_index("cp"),
            jnp.int32(kv_ranges.shape[1]),
            jnp.int32(kv_ranges.shape[2]),
            goes_up(),
        ]
    ).astype(jnp.int32)
    queries, keys, values = (
        array.reshape(token_rows, width_dev) for array in (query_rows, key_rows, value_rows)
    )
    head_counts = CHUNKS + (KEYS_MOVED,)
    assert sum(head_counts) == head_total and 2 * KEYS_MOVED == sum(CHUNKS)
    assert lax.axis_size("stretch") == 2
    bases = [sum(head_counts[:i]) for i in range(len(head_counts))]
    widths = [count * HEAD_DIM for count in head_counts]
    chunks = range(len(CHUNKS))
    last = len(CHUNKS)

    def float_shape(chunk):
        return jax.ShapeDtypeStruct((token_rows, widths[chunk]), jnp.float32)

    def payload_shape(chunk):
        return jax.ShapeDtypeStruct((token_rows + STAT_ROWS, widths[chunk]), jnp.bfloat16)

    stats_shape = jax.ShapeDtypeStruct((STAT_ROWS, BLOCK), jnp.float32)
    squares_shape = jax.ShapeDtypeStruct((8, BLOCK), jnp.float32)

    def run(name, kernel, chunk, microseconds, out_shape, smem, vmem, after=()):
        return pl.pallas_call(
            functools.partial(kernel, head_counts[chunk]),
            out_shape=out_shape,
            in_specs=[SMEM] * len(smem)
            + [VMEM] * len(vmem)
            + [pl.BlockSpec(memory_space=pl.ANY)] * len(after),
            out_specs=(VMEM,) * len(out_shape),
            compiler_params=PARAMS,
            cost_estimate=cost(microseconds),
            name=name,
        )(*smem, *vmem, *after)

    def block_shape(units):
        return jax.ShapeDtypeStruct((token_rows, units * HEAD_DIM), jnp.bfloat16)

    packed = pl.pallas_call(
        functools.partial(pack_kernel, CHUNKS, KEYS_MOVED),
        out_shape=(block_shape(head_total),) * 3
        + tuple(block_shape(units) for count in CHUNKS for units in (2 * count, count, count)),
        in_specs=[SMEM] + [pl.BlockSpec(memory_space=pltpu.HBM)] * 3,
        out_specs=(VMEM,) * (3 + 3 * len(CHUNKS)),
        scratch_shapes=[pltpu.SemaphoreType.DMA((3,))],
        compiler_params=pltpu.CompilerParams(vmem_limit_bytes=PACK_LIMIT),
        cost_estimate=cost(1.0),
        name="pack",
    )(place, queries, keys, values)
    queries, keys, values = packed[:3]
    prior_kv, hops = [], [[], []]
    for i in chunks:
        crossing, forward, backward = packed[3 * i + 3 : 3 * i + 6]
        prior_kv.append(exchanged(crossing))
        hops[0].append((round_trip(forward, True), round_trip(backward, False)))
    for i in chunks:
        forward, backward = hops[0][i]
        hops[1].append((round_trip(forward, True), round_trip(backward, False)))

    own_parts, near_parts, arrived = [], [], []
    gates, flags = pl.pallas_call(
        functools.partial(plan_kernel, pair_count),
        out_shape=(
            jax.ShapeDtypeStruct((8, width_dev), jnp.float32),
            jax.ShapeDtypeStruct((FLAGS,), jnp.int32),
        ),
        in_specs=[SMEM] * 3 + [VMEM],
        out_specs=(VMEM, SMEM),
        compiler_params=PARAMS,
        cost_estimate=cost(0.6),
        name="plan",
    )(place, kv_ranges, levels, gate_table)
    turn = ()
    for i in chunks:
        near = run(
            "near",
            functools.partial(near_kernel, base=bases[i], pair_count=pair_count),
            i,
            NEAR_COST[i],
            (float_shape(i), stats_shape) * 2,
            (flags,),
            (queries, keys, values, *hops[0][i], prior_kv[i]),
            turn,
        )
        own_parts.append(near[:2])
        near_parts.append(near[2:])
        far_payload, far_stats = run(
            "far",
            functools.partial(far_kernel, base=bases[i], pair_count=pair_count),
            i,
            FAR_COST[i],
            (payload_shape(i), stats_shape),
            (flags,),
            (keys, values, *hops[1][i], prior_kv[i]),
            (near[1],),
        )
        turn = (far_stats,)
        arrived.append(passed_up(far_payload, True))
    own_out, own_stats, next_payload = run(
        "keys_moved",
        functools.partial(
            keys_moved_kernel, base=bases[last], pair_count=pair_count, counts=CHUNKS
        ),
        last,
        KEYS_COST,
        (float_shape(last), stats_shape, payload_shape(last)),
        (flags,),
        (queries, keys, values, prior_kv[0], *[ref for hop in hops for pair in hop for ref in pair]),
        turn,
    )
    own_parts.append((own_out, own_stats))
    turn = (own_stats,)
    arrived.append(exchanged(next_payload))
    for i in chunks:
        relayed, relayed_stats = run(
            "relay",
            functools.partial(relay_kernel, axis=1),
            i,
            0.7,
            (payload_shape(i), stats_shape),
            (place,),
            (*near_parts[i], arrived[i]),
            turn,
        )
        turn = (relayed_stats,)
        arrived[i] = passed_up(relayed, i == 0)
    squares = jnp.zeros(squares_shape.shape, jnp.float32)
    finished = [None] * len(head_counts)
    for i in FINISH_ORDER:
        finished[i], squares = run(
            "finish",
            functools.partial(finish_kernel, axis=0 if i == last else 1, base=bases[i]),
            i,
            0.8,
            (float_shape(i), squares_shape),
            (place,),
            (*own_parts[i], arrived[i], gates, squares),
            turn,
        )
    device_count = lax.axis_size("tp")
    assert device_count & (device_count - 1) == 0
    shares = [squares]
    for distance in reversed(range(1, device_count)):
        route = [(i, i ^ distance) for i in range(device_count)]
        shares.append(lax.ppermute(squares, "tp", route))
    out = pl.pallas_call(
        functools.partial(scale_kernel, head_counts, float(HEADS * HEAD_DIM), device_count),
        out_shape=jax.ShapeDtypeStruct((token_rows, width_dev), jnp.bfloat16),
        in_specs=[VMEM] * (device_count + len(finished)),
        out_specs=VMEM,
        compiler_params=PARAMS,
        name="scale",
    )(*shares, *finished)
    return out.reshape(query_rows.shape)


def solution(mesh):
    in_specs = (
        P("stretch", "cp", "tp"),
        P("stretch", "cp", "tp"),
        P("stretch", "cp", "tp"),
        P(None, "tp"),
        P(),
        P(),
    )
    out_specs = P("stretch", "cp", "tp")
    return jax.shard_map(
        on_device, mesh=mesh, in_specs=in_specs, out_specs=out_specs, check_vma=False
    )
```

```python
import functools
import math

import jax
import jax.numpy as jnp
from jax import lax
from jax.experimental import pallas as pl
from jax.experimental.pallas import tpu as pltpu
from jax.sharding import PartitionSpec as P

HEADS = 48
HEAD_DIM = 128
BLOCK = 128
REACH = 2
CHUNKS = (5, 3)
KEYS_MOVED = 4
FINISH_ORDER = (2, 0, 1)
WRAP = True
NEAR_COST = (3.0, 1.8)
FAR_COST = (1.5, 0.9)
KEYS_COST = 2.0
PACK_LIMIT = 49 * 1024 * 1024
STAT_ROWS = 16
FLAGS = 64
HIDDEN = -1e30
EXPONENT_SCALE = math.log2(math.e) / math.sqrt(HEAD_DIM)


def exchanged(block):
    return lax.ppermute(block, "stretch", [(0, 1), (1, 0)])


def goes_up():
    return lax.axis_index("tp") < lax.axis_size("tp") // 2


def round_trip(block, forward):
    count, half = lax.axis_size("cp"), lax.axis_size("tp") // 2
    route = []
    for lane in range(half):
        cycle = [i * 2 * half + lane for i in range(count)]
        cycle += [i * 2 * half + half + lane for i in reversed(range(count))]
        route += zip(cycle, cycle[1:] + cycle[:1])
    if not forward:
        route = [(target, source) for source, target in route]
    return lax.ppermute(block, ("cp", "tp"), route)


def passed_up(block, wrap):
    count = lax.axis_size("cp")
    route = [(i, (i + 1) % count) for i in range(count if wrap else count - 1)]
    return lax.ppermute(block, "cp", route)


def head_columns(head):
    return slice(head * HEAD_DIM, (head + 1) * HEAD_DIM)


def stretch_rows(slot):
    return slice(slot * BLOCK, (slot + 1) * BLOCK)


def as_columns(rows):
    fill = jnp.zeros((BLOCK - rows.shape[0], BLOCK), jnp.float32)
    return jnp.transpose(jnp.concatenate([rows, fill], axis=0))


def put_stats(payload_ref, stats, token_rows):
    high = stats.astype(jnp.bfloat16)
    rest = stats - high.astype(jnp.float32)
    middle = rest.astype(jnp.bfloat16)
    low = (rest - middle.astype(jnp.float32)).astype(jnp.bfloat16)
    rows = slice(token_rows, token_rows + STAT_ROWS)
    for index, piece in enumerate((high, middle, low)):
        payload_ref[rows, head_columns(index)] = piece


def get_stats(payload_ref, token_rows):
    rows = slice(token_rows, token_rows + STAT_ROWS)
    pieces = [
        payload_ref[rows, head_columns(index)].astype(jnp.float32) for index in range(3)
    ]
    return (pieces[0] + pieces[1]) + pieces[2]


def shown(place_ref, ranges_ref, query_stretch, query_block, key_stretch, key_block):
    stretch_count, block_count = place_ref[2], place_ref[3]
    low, high = (
        ranges_ref[
            end,
            jnp.minimum(query_stretch, stretch_count - 1),
            jnp.minimum(query_block, block_count - 1),
            jnp.maximum(key_stretch, 0),
        ]
        for end in range(2)
    )
    exists = (
        (query_stretch < stretch_count)
        & (query_block < block_count)
        & (key_stretch >= 0)
        & (key_block >= 0)
    )
    return exists & (low <= key_block) & (key_block < high)


def attend(query, keys, values, seen):
    scores = lax.dot_general(
        keys, query, (((1,), (1,)), ((), ())), preferred_element_type=jnp.float32
    )
    blocks = [scores[stretch_rows(j)] for j in range(len(seen))]
    peak = jnp.full((1, BLOCK), HIDDEN, jnp.float32)
    for block, flag in zip(blocks, seen):
        block_peak = jnp.max(block, axis=0, keepdims=True)
        peak = jnp.maximum(peak, jnp.where(flag, block_peak, HIDDEN))
    shift = peak * EXPONENT_SCALE
    weights = [
        jnp.exp2(block * EXPONENT_SCALE - jnp.where(flag, shift, -HIDDEN))
        for block, flag in zip(blocks, seen)
    ]
    total = sum(jnp.sum(weight, axis=0, keepdims=True) for weight in weights)
    weights = jnp.concatenate([weight.astype(jnp.bfloat16) for weight in weights], axis=0)
    summed = jnp.dot(values, weights, preferred_element_type=jnp.float32)
    total = jnp.maximum(total, 1e-30)
    return summed * (1.0 / total), jnp.maximum(shift + jnp.log2(total), HIDDEN)


def pick(up, refs, *index):
    return jnp.where(up, refs[0][index], refs[1][index])


def pack_kernel(counts, keys_moved, place_ref, q_hbm, k_hbm, v_hbm, *refs):
    base = sum(counts)
    q_ref, k_ref, v_ref = refs[:3]
    outs, semaphores = refs[3:-1], refs[-1]
    copies = [
        pltpu.make_async_copy(source, target, semaphores.at[index])
        for index, (source, target) in enumerate(
            ((q_hbm, q_ref), (k_hbm, k_ref), (v_hbm, v_ref))
        )
    ]
    for copy in copies:
        copy.start()
    columns = [head_columns(head) for head in range(base + keys_moved)]
    moving = [(ref, part) for ref in (k_ref, v_ref) for part in columns[base:]]
    up = place_ref[4] == 1
    last_group = place_ref[0] > 0
    bounds = [sum(counts[:i]) for i in range(len(counts) + 1)]

    def fill(out, parts, source):
        for index, (ref, part) in enumerate(parts):
            if ref is source:
                out[:, head_columns(index)] = ref[:, part]

    for copy, source in zip(copies, (q_ref, k_ref, v_ref)):
        copy.wait()
        jobs = []
        for i, (start, stop) in enumerate(zip(bounds, bounds[1:])):
            own = columns[start:stop]
            jobs.append(
                (
                    *outs[3 * i : 3 * i + 3],
                    [(ref, part) for ref in (k_ref, v_ref) for part in own],
                    [(q_ref, part) for part in own],
                    moving[start:stop],
                )
            )

        @pl.when(up)
        def _():
            for _, forward_out, backward_out, _, queries, keys in jobs:
                fill(forward_out, keys, source)
                fill(backward_out, queries, source)

        @pl.when(jnp.logical_not(up))
        def _():
            for _, forward_out, backward_out, _, queries, keys in jobs:
                fill(forward_out, queries, source)
                fill(backward_out, keys, source)

        for cross_out, _, _, crossing, _, _ in jobs:
            fill(cross_out, crossing, source)

    @pl.when(last_group)
    def _():
        fill(outs[0], [(q_ref, part) for part in columns[base:]], q_ref)


def crossing_keys(own_k, own_v, prior_kv, base, head, head_count):
    own_columns = head_columns(base + head)
    keys = jnp.concatenate([own_k[:, own_columns], prior_kv[:, head_columns(head)]], axis=0)
    values = jnp.concatenate(
        [own_v[:, own_columns], prior_kv[:, head_columns(head_count + head)]], axis=0
    )
    return keys, jnp.transpose(values)


def plan_kernel(pair_count, place_ref, ranges_ref, levels_ref, gate_table, *rest):
    gates_out, flags_out = rest[-2:]
    gates = gate_table[...].astype(jnp.float32)
    level_ids = lax.broadcasted_iota(jnp.int32, gates.shape, 0)
    gates_out[...] = jnp.zeros_like(gates_out)
    for slot in range(pair_count):
        level = levels_ref[place_ref[0] * pair_count + slot]
        gates_out[slot : slot + 1, :] = jnp.sum(
            jnp.where(level_ids == level, gates, 0.0), axis=0, keepdims=True
        )
    group, position = place_ref[0], place_ref[1]
    flags_out[0] = place_ref[4]
    index = 1
    for distance in range(REACH + 1):
        for slot in range(pair_count):
            for behind in range(2):
                for key_slot in range(pair_count):
                    flag = shown(
                        place_ref,
                        ranges_ref,
                        group * pair_count + slot,
                        position + distance,
                        (group - behind) * pair_count + key_slot,
                        position,
                    )
                    flags_out[index] = flag.astype(jnp.int32)
                    index += 1
    for ahead in range(2):
        for slot in range(pair_count):
            for distance in range(REACH + 1):
                for key_slot in range(pair_count):
                    flag = shown(
                        place_ref,
                        ranges_ref,
                        (group + ahead) * pair_count + slot,
                        position,
                        group * pair_count + key_slot,
                        position - distance,
                    )
                    flags_out[index] = flag.astype(jnp.int32)
                    index += 1


def crossing_flags(flags_ref, distance, slot, pair_count):
    base = 1 + (distance * pair_count + slot) * 2 * pair_count
    return [flags_ref[base + j] == 1 for j in range(2 * pair_count)]


def moved_flags(flags_ref, ahead, slot, pair_count):
    count = (REACH + 1) * pair_count
    base = 1 + count * 2 * pair_count + (ahead * pair_count + slot) * count
    return [flags_ref[base + j] == 1 for j in range(count)]


def far_kernel(
    head_count, flags_ref, own_k, own_v, forward_q, backward_q, prior_kv, *rest,
    base, pair_count,
):
    far_payload, far_stats = rest[-2:]
    up = flags_ref[0] == 1
    seen = [crossing_flags(flags_ref, 2, slot, pair_count) for slot in range(pair_count)]
    stats = [jnp.zeros((1, BLOCK), jnp.float32)] * STAT_ROWS
    for head in range(head_count):
        columns = head_columns(head)
        keys, values = crossing_keys(own_k, own_v, prior_kv, base, head, head_count)
        for slot in range(pair_count):
            rows = stretch_rows(slot)
            query = pick(up, (backward_q, forward_q), rows, columns)
            attended, stats[slot * head_count + head] = attend(query, keys, values, seen[slot])
            far_payload[rows, columns] = attended.astype(jnp.bfloat16)
    far_stats[...] = jnp.concatenate(stats, axis=0)
    put_stats(far_payload, far_stats[...], pair_count * BLOCK)


def near_kernel(
    head_count, flags_ref, own_q, own_k, own_v, forward_q, backward_q, prior_kv,
    *rest, base, pair_count,
):
    own_out, own_stats, near_out, near_stats = rest[-4:]
    up = flags_ref[0] == 1
    seen = {
        (distance, slot): crossing_flags(flags_ref, distance, slot, pair_count)
        for distance in range(2)
        for slot in range(pair_count)
    }
    own_stats[...] = jnp.zeros_like(own_stats)
    near_stats[...] = jnp.zeros_like(near_stats)
    for head in range(head_count):
        columns = head_columns(head)
        keys, values = crossing_keys(own_k, own_v, prior_kv, base, head, head_count)
        for slot in range(pair_count):
            rows = stretch_rows(slot)
            index = slot * head_count + head
            query = pick(up, (backward_q, forward_q), rows, columns)
            near_out[rows, columns], near_stats[index : index + 1, :] = attend(
                query, keys, values, seen[1, slot]
            )
            query = own_q[rows, head_columns(base + head)]
            own_out[rows, columns], own_stats[index : index + 1, :] = attend(
                query, keys, values, seen[0, slot]
            )


def keys_moved_kernel(
    head_count, flags_ref, own_q, own_k, own_v, next_q, *rest, base, pair_count, counts
):
    own_out, own_stats, next_payload = rest[-3:]
    up = flags_ref[0] == 1
    parts = len(counts)
    came = [
        [rest[2 * (hop * parts + part) : 2 * (hop * parts + part) + 2] for part in range(parts)]
        for hop in range(REACH)
    ]

    def moved_block(hop, unit):
        part = 0
        while unit >= counts[part]:
            unit -= counts[part]
            part += 1
        return pick(up, came[hop][part], slice(None), head_columns(unit))

    seen = {
        (ahead, slot): moved_flags(flags_ref, ahead, slot, pair_count)
        for ahead in range(2)
        for slot in range(pair_count)
    }
    own_stats[...] = jnp.zeros_like(own_stats)
    next_stats = [jnp.zeros((1, BLOCK), jnp.float32)] * STAT_ROWS
    for head in range(head_count):
        columns, own_columns = head_columns(head), head_columns(base + head)
        keys = jnp.concatenate(
            [own_k[:, own_columns]] + [moved_block(hop, head) for hop in range(REACH)], axis=0
        )
        values = jnp.transpose(
            jnp.concatenate(
                [own_v[:, own_columns]]
                + [moved_block(hop, head_count + head) for hop in range(REACH)],
                axis=0,
            )
        )
        for slot in range(pair_count):
            rows = stretch_rows(slot)
            index = slot * head_count + head
            attended, next_stats[index] = attend(
                next_q[rows, columns], keys, values, seen[1, slot]
            )
            next_payload[rows, columns] = attended.astype(jnp.bfloat16)
            own_out[rows, columns], own_stats[index : index + 1, :] = attend(
                own_q[rows, own_columns], keys, values, seen[0, slot]
            )
    put_stats(next_payload, jnp.concatenate(next_stats, axis=0), pair_count * BLOCK)


def joined(sender_index, local_out, local_stats, payload_ref, head_count):
    token_rows = local_out.shape[0]
    local_log = local_stats[...]
    remote_log = jnp.where(sender_index > 0, get_stats(payload_ref, token_rows), HIDDEN)
    top = jnp.maximum(local_log, remote_log)
    local_weight = jnp.exp2(local_log - top)
    remote_weight = jnp.exp2(remote_log - top)
    both = local_weight + remote_weight
    scale = 1.0 / both
    local_weight = local_weight * scale
    remote_weight = remote_weight * scale
    parts = {}
    for slot in range(token_rows // BLOCK):
        for head in range(head_count):
            index = slot * head_count + head
            rows, columns = stretch_rows(slot), head_columns(head)
            parts[slot, head] = (
                local_out[rows, columns] * local_weight[index : index + 1]
                + payload_ref[rows, columns].astype(jnp.float32)
                * remote_weight[index : index + 1]
            )
    return parts, top + jnp.log2(both)


def relay_kernel(
    head_count, place_ref, local_out, local_stats, payload_in, *rest, axis
):
    payload_out, stats_out = rest[-2:]
    parts, log_total = joined(place_ref[axis], local_out, local_stats, payload_in, head_count)
    for (slot, head), part in parts.items():
        payload_out[stretch_rows(slot), head_columns(head)] = part.astype(jnp.bfloat16)
    stats_out[...] = log_total
    put_stats(payload_out, log_total, local_out.shape[0])


def finish_kernel(
    head_count, place_ref, local_out, local_stats, payload_in, gates, squares_in, *rest, axis, base
):
    out, squares_out = rest[-2:]
    parts, _ = joined(place_ref[axis], local_out, local_stats, payload_in, head_count)
    squares_out[...] = squares_in[...]
    for slot in range(local_out.shape[0] // BLOCK):
        total = jnp.zeros((1, BLOCK), jnp.float32)
        for head in range(head_count):
            part = parts[slot, head]
            total = total + jnp.sum(part * part, axis=0, keepdims=True)
            gate_row = gates[slot : slot + 1, head_columns(base + head)]
            out[stretch_rows(slot), head_columns(head)] = jnp.transpose(part) * gate_row
        squares_out[slot : slot + 1, :] += total


def scale_kernel(head_counts, feature_count, device_count, *refs):
    squares = sum(ref[...] for ref in refs[:device_count])
    parts = refs[device_count:-3]
    out_hbm, out, semaphores = refs[-3:]
    copies = []
    factors = as_columns(lax.rsqrt(squares / feature_count + 1e-06))
    for slot in range(out.shape[0] // BLOCK):
        rows = stretch_rows(slot)
        factor = factors[:, slot : slot + 1]
        base = 0
        for part, head_count in zip(parts, head_counts):
            for head in range(head_count):
                out[rows, head_columns(base + head)] = (
                    part[rows, head_columns(head)] * factor
                ).astype(jnp.bfloat16)
            base += head_count
        copies.append(pltpu.make_async_copy(out.at[rows], out_hbm.at[rows], semaphores.at[slot]))
        copies[-1].start()
    for copy in copies:
        copy.wait()


def cost(microseconds):
    return pl.CostEstimate(
        flops=int(microseconds * 1e9), bytes_accessed=int(microseconds * 1e6), transcendentals=0
    )


SMEM = pl.BlockSpec(memory_space=pltpu.SMEM)
VMEM = pl.BlockSpec(memory_space=pltpu.VMEM)
PARAMS = pltpu.CompilerParams(vmem_limit_bytes=32 * 1024 * 1024)


def on_device(query_rows, key_rows, value_rows, gate_table, levels, kv_ranges):
    pair_count, row_count, width_dev = query_rows.shape
    assert row_count == BLOCK
    token_rows = pair_count * row_count
    head_total = width_dev // HEAD_DIM
    place = jnp.stack(
        [
            lax.axis_index("stretch"),
            lax.axis_index("cp"),
            jnp.int32(kv_ranges.shape[1]),
            jnp.int32(kv_ranges.shape[2]),
            goes_up(),
        ]
    ).astype(jnp.int32)
    queries, keys, values = (
        array.reshape(token_rows, width_dev) for array in (query_rows, key_rows, value_rows)
    )
    head_counts = CHUNKS + (KEYS_MOVED,)
    assert sum(head_counts) == head_total and 2 * KEYS_MOVED == sum(CHUNKS)
    assert lax.axis_size("stretch") == 2
    bases = [sum(head_counts[:i]) for i in range(len(head_counts))]
    widths = [count * HEAD_DIM for count in head_counts]
    chunks = range(len(CHUNKS))
    last = len(CHUNKS)

    def float_shape(chunk):
        return jax.ShapeDtypeStruct((token_rows, widths[chunk]), jnp.float32)

    def payload_shape(chunk):
        return jax.ShapeDtypeStruct((token_rows + STAT_ROWS, widths[chunk]), jnp.bfloat16)

    stats_shape = jax.ShapeDtypeStruct((STAT_ROWS, BLOCK), jnp.float32)
    squares_shape = jax.ShapeDtypeStruct((8, BLOCK), jnp.float32)

    def run(name, kernel, chunk, microseconds, out_shape, smem, vmem, after=()):
        return pl.pallas_call(
            functools.partial(kernel, head_counts[chunk]),
            out_shape=out_shape,
            in_specs=[SMEM] * len(smem)
            + [VMEM] * len(vmem)
            + [pl.BlockSpec(memory_space=pl.ANY)] * len(after),
            out_specs=(VMEM,) * len(out_shape),
            compiler_params=PARAMS,
            cost_estimate=cost(microseconds),
            name=name,
        )(*smem, *vmem, *after)

    def block_shape(units):
        return jax.ShapeDtypeStruct((token_rows, units * HEAD_DIM), jnp.bfloat16)

    packed = pl.pallas_call(
        functools.partial(pack_kernel, CHUNKS, KEYS_MOVED),
        out_shape=(block_shape(head_total),) * 3
        + tuple(block_shape(units) for count in CHUNKS for units in (2 * count, count, count)),
        in_specs=[SMEM] + [pl.BlockSpec(memory_space=pltpu.HBM)] * 3,
        out_specs=(VMEM,) * (3 + 3 * len(CHUNKS)),
        scratch_shapes=[pltpu.SemaphoreType.DMA((3,))],
        compiler_params=pltpu.CompilerParams(vmem_limit_bytes=PACK_LIMIT),
        cost_estimate=cost(1.0),
        name="pack",
    )(place, queries, keys, values)
    queries, keys, values = packed[:3]
    prior_kv, hops = [], [[], []]
    for i in chunks:
        crossing, forward, backward = packed[3 * i + 3 : 3 * i + 6]
        prior_kv.append(exchanged(crossing))
        hops[0].append((round_trip(forward, True), round_trip(backward, False)))
    for i in chunks:
        forward, backward = hops[0][i]
        hops[1].append((round_trip(forward, True), round_trip(backward, False)))

    own_parts, near_parts, arrived = [], [], []
    gates, flags = pl.pallas_call(
        functools.partial(plan_kernel, pair_count),
        out_shape=(
            jax.ShapeDtypeStruct((8, width_dev), jnp.float32),
            jax.ShapeDtypeStruct((FLAGS,), jnp.int32),
        ),
        in_specs=[SMEM] * 3 + [VMEM],
        out_specs=(VMEM, SMEM),
        compiler_params=PARAMS,
        cost_estimate=cost(0.6),
        name="plan",
    )(place, kv_ranges, levels, gate_table)
    turn = ()
    for i in chunks:
        near = run(
            "near",
            functools.partial(near_kernel, base=bases[i], pair_count=pair_count),
            i,
            NEAR_COST[i],
            (float_shape(i), stats_shape) * 2,
            (flags,),
            (queries, keys, values, *hops[0][i], prior_kv[i]),
            turn,
        )
        own_parts.append(near[:2])
        near_parts.append(near[2:])
        far_payload, far_stats = run(
            "far",
            functools.partial(far_kernel, base=bases[i], pair_count=pair_count),
            i,
            FAR_COST[i],
            (payload_shape(i), stats_shape),
            (flags,),
            (keys, values, *hops[1][i], prior_kv[i]),
            (near[1],),
        )
        turn = (far_stats,)
        arrived.append(passed_up(far_payload, True))
    own_out, own_stats, next_payload = run(
        "keys_moved",
        functools.partial(
            keys_moved_kernel, base=bases[last], pair_count=pair_count, counts=CHUNKS
        ),
        last,
        KEYS_COST,
        (float_shape(last), stats_shape, payload_shape(last)),
        (flags,),
        (queries, keys, values, prior_kv[0], *[ref for hop in hops for pair in hop for ref in pair]),
        turn,
    )
    own_parts.append((own_out, own_stats))
    turn = (own_stats,)
    arrived.append(exchanged(next_payload))
    for i in chunks:
        relayed, relayed_stats = run(
            "relay",
            functools.partial(relay_kernel, axis=1),
            i,
            0.7,
            (payload_shape(i), stats_shape),
            (place,),
            (*near_parts[i], arrived[i]),
            turn,
        )
        turn = (relayed_stats,)
        arrived[i] = passed_up(relayed, i == 0)
    squares = jnp.zeros(squares_shape.shape, jnp.float32)
    finished = [None] * len(head_counts)
    for i in FINISH_ORDER:
        finished[i], squares = run(
            "finish",
            functools.partial(finish_kernel, axis=0 if i == last else 1, base=bases[i]),
            i,
            0.8,
            (float_shape(i), squares_shape),
            (place,),
            (*own_parts[i], arrived[i], gates, squares),
            turn,
        )
    device_count = lax.axis_size("tp")
    assert device_count & (device_count - 1) == 0
    shares = [squares]
    for distance in reversed(range(1, device_count)):
        route = [(i, i ^ distance) for i in range(device_count)]
        shares.append(lax.ppermute(squares, "tp", route))
    out = pl.pallas_call(
        functools.partial(scale_kernel, head_counts, float(HEADS * HEAD_DIM), device_count),
        out_shape=jax.ShapeDtypeStruct((token_rows, width_dev), jnp.bfloat16),
        in_specs=[VMEM] * (device_count + len(finished)),
        out_specs=pl.BlockSpec(memory_space=pltpu.HBM),
        scratch_shapes=[
            pltpu.VMEM((token_rows, width_dev), jnp.bfloat16),
            pltpu.SemaphoreType.DMA((pair_count,)),
        ],
        compiler_params=PARAMS,
        name="scale",
    )(*shares, *finished)
    return out.reshape(query_rows.shape)


def solution(mesh):
    in_specs = (
        P("stretch", "cp", "tp"),
        P("stretch", "cp", "tp"),
        P("stretch", "cp", "tp"),
        P(None, "tp"),
        P(),
        P(),
    )
    out_specs = P("stretch", "cp", "tp")
    return jax.shard_map(
        on_device, mesh=mesh, in_specs=in_specs, out_specs=out_specs, check_vma=False
    )
```
